32 devices in a mesh: grp: 2 (over y), ex: 4 (over z), feat: 4 (over x, core).
Axes of the slice: x: 2, y: 2, z: 4, core: 2. Of those that a mesh axis runs over, the one named last changes fastest.
Arguments:
- slab_grads: bfloat16 [4096, 4096], P(('grp', 'ex'), 'feat'), parts along dimension 0, may hold values from -6 to 6
- query_grads: bfloat16 [4096, 4096], P(('grp', 'feat'), 'ex'), parts along dimension 0, may hold values from -0.09375 to 0.09375
- example_weights: float32 [4096], P(('grp', 'ex')), parts along dimension 0, may hold values from 0.2 to 2
- tile_owner: int32 [8, 168, 2], P(('grp', 'feat')), parts along dimension 0, may hold values from -1 to 31, as said below
Outputs:
- gram: float32 [8, 168, 128, 128], P(('grp', 'feat'), 'ex'), parts along dimension 0
- scores: float32 [4096, 2048], P(('grp', 'feat'), 'ex'), parts along dimension 0
The draws below stay inside these ranges and needn't reach their ends.
There are 2 independent parts, one for each index of `grp`. The reference program is written for one: setup_inputs(seed, part) draws one part's arguments, and reference() takes and returns one part's arrays. A program takes and returns all parts, laid end to end along the dimension named above; each array names one. Nothing has to cross between parts.
Inputs may be any that keep to these rules, and one draw needn't show every extreme that they name: `tile_owner`: each slot holds a pair (a, b) with a <= b of the 32 feature blocks, or (-1, -1) when empty; every such pair stands in exactly one slot; one column has min(168, 528) live slots.
All inputs are finite; a program needn't handle non-finite values.
Results may differ from the reference program's by a relative error of at most 0.008.
Values may be sent and summed in bfloat16 or wider, within the bound.
No kernel may reach another device: no remote copies, remote signals or barrier semaphores. Data moves between devices by JAX's collectives and lax.ppermute only.
A program may use at most 64 MiB of HBM per device.

```python
import math
import jax
import jax.numpy as jnp
import numpy as np
from jax import lax

K = 4096
B = 128
TOK_DEV = 512
NB = 32
PAIRS = 528
COLUMNS = 4
SLOTS = 168
ROWS = 2048
QUERIES = 2048
N_EX = 4


def draw_tile_owner(key, part):
    key = jax.random.fold_in(key, 5)
    key_order, key_busy, key_heavy, key_spread = jax.random.split(key, 4)
    first, second = np.triu_indices(NB)
    pairs = jnp.stack([jnp.asarray(first, jnp.int32), jnp.asarray(second, jnp.int32)], 1)
    shuffled = pairs[jax.random.permutation(key_order, PAIRS)]
    busiest = jax.random.randint(key_busy, (), 0, COLUMNS)
    full_count = min(SLOTS, PAIRS)
    heavy_slots = busiest * SLOTS + jax.random.permutation(key_heavy, SLOTS)[:full_count]
    remaining = PAIRS - full_count
    free_spots = jax.random.permutation(key_spread, (COLUMNS - 1) * SLOTS)[:remaining]
    column = free_spots // SLOTS
    column = column + (column >= busiest).astype(jnp.int32)
    other_slots = column * SLOTS + free_spots % SLOTS
    slot_table = jnp.full((COLUMNS * SLOTS, 2), -1, jnp.int32)
    slot_table = slot_table.at[heavy_slots].set(shuffled[:full_count])
    slot_table = slot_table.at[other_slots].set(shuffled[full_count:])
    return slot_table.reshape(COLUMNS, SLOTS, 2)


def shard_levels(rng, extent, pieces, least, high):
    gain = 1.0
    for position, blocks in pieces:
        steps = jax.random.uniform(jax.random.fold_in(jax.random.fold_in(rng, 6), position), (blocks,), jnp.float32, least / len(pieces), high / len(pieces))
        gain = gain * jnp.repeat(jnp.exp(steps), extent[position] // blocks).reshape((-1,) + (1,) * (len(extent) - 1 - position))
    return gain


def gaussian(own_key, shape, deviation, reach, cuts=(), kind=jnp.bfloat16):
    result = jax.random.normal(own_key, shape, jnp.float32) * deviation
    if len(cuts) > 0:
        result = shard_levels(own_key, shape, cuts, -0.22, 0.18) * result
    return jnp.clip(result, min=-reach, max=reach).astype(kind)


def setup_inputs(seed: int = 0, part: int = 0) -> dict:
    arg_keys = jax.random.split(jax.random.key(seed), 5)
    part_keys = jax.random.split(jax.random.fold_in(arg_keys[4], part), 5)
    slab_grads = gaussian(part_keys[0], (ROWS, K), 1.0, 6.0, ((0, 4), (1, 4)))
    query_grads = gaussian(part_keys[1], (QUERIES, K), K ** -0.5, 0.09375, ((0, 4), (1, 4)))
    example_weights = jnp.clip(jnp.exp(math.log(2.0) - 2.3025851 * jax.random.uniform(part_keys[2], (ROWS,), jnp.float32) ** shard_levels(part_keys[2], (ROWS,), ((0, 4),), -0.2, 0.2)), 0.2, 2.0)
    tile_owner = draw_tile_owner(jax.random.fold_in(jax.random.fold_in(arg_keys[4], part), 71), part)
    return dict(slab_grads=slab_grads, query_grads=query_grads, example_weights=example_weights, tile_owner=tile_owner)


def reference(slab_grads, query_grads, example_weights, tile_owner):
    shards = slab_grads.reshape(N_EX, TOK_DEV, K)

    def shard_step(running, shard):
        partial_value = jnp.dot(shard.T, shard, preferred_element_type=jnp.float32).astype(jnp.bfloat16)
        partial_value = lax.optimization_barrier(partial_value)
        return running + partial_value.astype(jnp.float32), None

    total, _ = lax.scan(shard_step, jnp.zeros((K, K), jnp.float32), shards)
    total = total / ROWS
    blocks = total.reshape(NB, B, NB, B).transpose(0, 2, 1, 3)
    first = tile_owner[..., 0]
    second = tile_owner[..., 1]
    picked = blocks[jnp.maximum(first, 0), jnp.maximum(second, 0)]
    gram = jnp.where((first >= 0)[..., None, None], picked, jnp.float32(0.0))
    scores = jnp.dot(query_grads, slab_grads.T, preferred_element_type=jnp.float32) * example_weights[None, :]
    return gram, scores
```

```python
import functools
import math

import jax
import jax.numpy as jnp
from jax import lax
from jax.experimental import pallas as pl
from jax.experimental.pallas import tpu as pltpu
from jax.sharding import PartitionSpec as P

B = 128


def select_blocks(blocks3, indices):
    block_ids = lax.broadcasted_iota(jnp.int32, (indices.shape[0], blocks3.shape[1]), 1)
    onehot = (indices[:, None] == block_ids).astype(jnp.bfloat16)
    chosen = jnp.einsum("tnb,gn->tgb", blocks3, onehot, preferred_element_type=jnp.float32)
    return chosen.astype(jnp.bfloat16)


def tile_terms(blocks3, subset):
    group_size = math.gcd(subset.shape[0], 8)
    groups = subset.reshape(-1, group_size, 2)

    def group_tiles(group):
        left_block = select_blocks(blocks3, group[:, 0])
        right_block = select_blocks(blocks3, group[:, 1])
        product = jnp.einsum(
            "tsi,tsj->sij", left_block, right_block, preferred_element_type=jnp.float32
        )
        return jnp.where((group[:, 0] >= 0)[:, None, None], product, jnp.float32(0.0))

    return lax.map(group_tiles, groups).reshape(-1, blocks3.shape[2], blocks3.shape[2])


def local_any(slab_grads, query_grads, example_weights, tile_owner):
    tile_table = tile_owner[0]
    tok_count = slab_grads.shape[0]
    slab_full = lax.all_gather(slab_grads, "feat", axis=1, tiled=True)
    blocks3 = slab_full.reshape(tok_count, slab_full.shape[1] // B, B)
    row_total = tok_count * lax.axis_size("ex")
    summed = lax.psum_scatter(
        tile_terms(blocks3, tile_table).astype(jnp.bfloat16), "ex", scatter_dimension=0, tiled=True
    ).astype(jnp.float32)
    gram = (summed / row_total)[None]
    summed = lax.dot_general(
        lax.all_gather(query_grads, "ex", axis=1, tiled=True),
        slab_full,
        (((1,), (1,)), ((), ())),
        preferred_element_type=jnp.float32,
    )
    scores = summed * example_weights[None, :]
    return (gram, scores)


PAIR = ((0, 1), (1, 0), (2, 3), (3, 2))
INNER = ((1, 2), (2, 1))
TO_END = ((1, 0), (2, 3))
TO_MID = ((0, 1), (3, 2))
END_TO_FAR_MID = ((0, 2), (3, 1))
MID_TO_FAR_END = ((1, 3), (2, 0))
CORE = ((0, 1), (1, 0), (2, 3), (3, 2))
ACROSS = ((0, 2), (2, 0), (1, 3), (3, 1))


def slot_kernel(slots, carry, final, place, table, *refs):
    refs = list(refs)
    pieces = [refs.pop(0) for _ in range(2 * len(slots))]
    pieces = [p for p in pieces]
    queries = refs.pop(0), refs.pop(0)
    acc_in = refs.pop(0) if carry else None
    outs = [refs.pop(0) for _ in range(2 if final else 1)]
    scored = [refs.pop(0) for _ in range(len(set(s for s, _ in slots)))]
    rows, turned, query, row_sem, query_sem = refs
    tiles = table.shape[0]

    copies = []
    at = 0
    for i, (_, count) in enumerate(slots):
        for half in range(2):
            copies.append(
                pltpu.make_async_copy(
                    pieces[2 * i + half], rows.at[half, pl.ds(at, count)], row_sem.at[2 * i + half]
                )
            )
        at += count
    for copy in copies:
        copy.start()
    query_copies = [
        pltpu.make_async_copy(queries[j], query.at[j], query_sem.at[j]) for j in range(2)
    ]
    middle = place[0] == 1

    @pl.when(middle)
    def _():
        for copy in query_copies:
            copy.start()

    for copy in copies:
        copy.wait()

    for block in range(32):
        turned[block] = rows[block // 16, :, (block % 16) * B : (block % 16 + 1) * B].T

    def one(tile, _):
        left = table[tile, 0]
        right = table[tile, 1]
        product = jnp.dot(
            turned[left],
            rows[right // 16, :, pl.ds(pl.multiple_of((right % 16) * B, B), B)],
            preferred_element_type=jnp.float32,
        )
        if carry:
            product += acc_in[tile]
        return product

    def store(tile, _):
        outs[0][tile] = one(tile, _)
        return 0

    def store_sibling(tile, _):
        outs[0][tile] = one(tile, _).astype(outs[0].dtype)
        return 0

    def store_own(tile, _):
        outs[1][tile] = one(tile + tiles // 2, _)
        return 0

    if final:
        lax.fori_loop(0, tiles // 2, store_sibling, 0, unroll=6)
        lax.fori_loop(0, tiles // 2, store_own, 0, unroll=6)
    else:
        lax.fori_loop(0, tiles, store, 0, unroll=6)

    @pl.when(middle)
    def _():
        for copy in query_copies:
            copy.wait()
        group = query.shape[1] // 4
        quarter = query.shape[2]
        start = 0
        for n, ref in enumerate(scored):
            count = ref.shape[2]
            for j in range(2):
                total = None
                for k in range(4):
                    spot = place[1 + k]
                    term = lax.dot_general(
                        query[j, k * group : (k + 1) * group, :],
                        rows[
                            spot // 2,
                            start : start + count,
                            pl.ds(pl.multiple_of((spot % 2) * quarter, quarter), quarter),
                        ],
                        (((1,), (1,)), ((), ())),
                        preferred_element_type=jnp.float32,
                    )
                    total = term if total is None else total + term
                ref[j] = total.astype(ref.dtype)
            start += count


def slot_call(place, table, slots, pieces, queries, acc=None, final=False):
    tiles = table.shape[0]
    total = sum(count for _, count in slots)
    wide = pieces[0].shape[1]
    names = sorted(set(s for s, _ in slots))
    counts = [sum(c for s, c in slots if s == n) for n in names]
    group = queries[0].shape[0] // 4
    if final:
        outs = [
            jax.ShapeDtypeStruct((tiles // 2, B, B), jnp.bfloat16),
            jax.ShapeDtypeStruct((tiles // 2, B, B), jnp.float32),
        ]
    else:
        outs = [jax.ShapeDtypeStruct((tiles, B, B), jnp.float32)]
    outs += [jax.ShapeDtypeStruct((2, group, c), jnp.bfloat16) for c in counts]
    carry = acc is not None
    smem = pl.BlockSpec(memory_space=pltpu.SMEM)
    vmem = pl.BlockSpec(memory_space=pltpu.VMEM)
    anywhere = pl.BlockSpec(memory_space=pl.ANY)
    flops = 2 * tiles * B * B * total + 2 * 2 * group * total * 2 * wide
    return pl.pallas_call(
        functools.partial(slot_kernel, slots, carry, final),
        out_shape=outs,
        in_specs=[smem, smem]
        + [anywhere] * (len(pieces) + 2)
        + ([vmem] if carry else []),
        out_specs=[vmem] * len(outs),
        scratch_shapes=[
            pltpu.VMEM((2, total, wide), jnp.bfloat16),
            pltpu.VMEM((2 * wide // B, B, total), jnp.bfloat16),
            pltpu.VMEM((2,) + queries[0].shape, jnp.bfloat16),
            pltpu.SemaphoreType.DMA((len(pieces),)),
            pltpu.SemaphoreType.DMA((2,)),
        ],
        compiler_params=pltpu.CompilerParams(vmem_limit_bytes=44 * 2**20),
        cost_estimate=pl.CostEstimate(
            flops=flops, bytes_accessed=8 * total * wide, transcendentals=0
        ),
    )(place, table, *pieces, *queries, *([acc] if carry else []))


def local_line(slab_grads, query_grads, example_weights, tile_owner):
    count, quarter = slab_grads.shape
    half, piece = count // 2, count // 4
    e = lax.axis_index("ex")
    f = lax.axis_index("feat")
    core = f % 2
    middle = jnp.logical_or(e == 1, e == 2)
    late = (e >= 2).astype(jnp.int32)

    def planes(which):
        return [(p * 4 + g, p * 4 + (g ^ 2)) for p in which for g in range(4)]

    def cores(which):
        return [(p * 4 + g, p * 4 + (g ^ 1)) for p in which for g in range(4)]

    def move(values, pairs):
        return [lax.ppermute(v, "ex", pairs) for v in values]

    def across(values):
        return [lax.ppermute(v, "feat", ACROSS) for v in values]

    keep = lax.dynamic_slice(slab_grads, (core * half, 0), (half, quarter))
    give = lax.dynamic_slice(slab_grads, ((1 - core) * half, 0), (half, quarter))
    own = jnp.concatenate([keep, lax.ppermute(give, "feat", CORE)], axis=1)
    own2 = [own[:piece], own[piece:]]

    near = move(own2, PAIR)
    inner = move(own2, INNER)
    outer = move(near, INNER)
    second = [jnp.where(middle, a, b) for a, b in zip(inner, move(inner, TO_END))]
    third = [jnp.where(middle, a, b) for a, b in zip(outer, move(outer, TO_END))]

    own_x = across([own])
    near_x = across(near)
    second_x = across(second)
    third_x = across(third)

    q_half = query_grads.shape[0] // 2
    mine = lax.dynamic_slice(query_grads, (late * q_half, 0), (q_half, quarter))
    other = lax.dynamic_slice(query_grads, ((1 - late) * q_half, 0), (q_half, quarter))
    queries = jnp.concatenate(
        [
            mine,
            lax.ppermute(mine, "ex", TO_MID),
            lax.ppermute(other, "ex", INNER),
            lax.ppermute(other, "ex", END_TO_FAR_MID),
        ],
        axis=0,
    )
    queries = (queries, lax.ppermute(queries, ("ex", "feat"), cores((1, 2))))

    slots = tile_owner.shape[1] // 4
    own_tiles = lax.dynamic_slice(tile_owner[0], (e * slots, 0), (slots, 2))
    tiles = jnp.concatenate([lax.ppermute(own_tiles, "feat", CORE), own_tiles], axis=0)
    blocks = quarter // B
    tiles = jnp.maximum(tiles, 0)
    table = ((tiles // blocks) ^ f) * blocks + tiles % blocks
    order = jnp.where(e == 2, jnp.array([2, 3, 1, 0]), jnp.array([1, 0, 2, 3])).astype(jnp.int32)
    place = jnp.concatenate([middle.astype(jnp.int32)[None], order ^ f])

    acc, r_own, r_near = slot_call(
        place,
        table,
        ((0, half), (1, piece), (1, piece)),
        [own, own_x[0], near[0], near_x[0], near[1], near_x[1]],
        queries,
    )
    acc, r_second = slot_call(
        place,
        table,
        ((2, piece), (2, piece)),
        [second[0], second_x[0], second[1], second_x[1]],
        queries,
        acc,
    )
    for_sibling, for_own, r_third = slot_call(
        place,
        table,
        ((3, piece), (3, piece)),
        [third[0], third_x[0], third[1], third_x[1]],
        queries,
        acc,
        final=True,
    )

    gram = for_own + lax.ppermute(for_sibling, "feat", CORE).astype(jnp.float32)
    gram = gram / (count * 4)
    gram = jnp.where((own_tiles[:, 0] >= 0)[:, None, None], gram, jnp.float32(0.0))

    to_end = lax.ppermute(r_near, "ex", TO_END)
    to_mid = lax.ppermute(r_second, "ex", INNER)
    to_far = lax.ppermute(r_third, "ex", MID_TO_FAR_END)
    first = jnp.where(middle, r_own, to_end)
    rest = jnp.where(middle, to_mid, to_far)
    low = jnp.where(late == 1, rest, first)
    high = jnp.where(late == 1, first, rest)
    both = jnp.concatenate([low, high], axis=1)
    got = lax.ppermute(both[1], "feat", CORE)
    left = jnp.where(core == 0, both[0], got)
    right = jnp.where(core == 0, got, both[0])
    scores = jnp.concatenate([left, right], axis=1).astype(jnp.float32)
    return gram[None], scores * example_weights[None, :]


def solution(mesh):
    placed = (
        P(("grp", "ex"), "feat"),
        P(("grp", "feat"), "ex"),
        P(("grp", "ex")),
        P(("grp", "feat"), None, None),
    )

    line = mesh.shape["ex"] == 4 and mesh.shape["feat"] == 4
    return jax.shard_map(
        local_line if line else local_any,
        mesh=mesh,
        in_specs=placed,
        out_specs=(P(("grp", "feat"), "ex", None, None), P(("grp", "feat"), "ex")),
        check_vma=False,
    )
```

```python
import math

import jax
import jax.numpy as jnp
from jax import lax
from jax.experimental import pallas as pl
from jax.experimental.pallas import tpu as pltpu
from jax.sharding import PartitionSpec as P

B = 128


def select_blocks(blocks3, indices):
    block_ids = lax.broadcasted_iota(jnp.int32, (indices.shape[0], blocks3.shape[1]), 1)
    onehot = (indices[:, None] == block_ids).astype(jnp.bfloat16)
    chosen = jnp.einsum("tnb,gn->tgb", blocks3, onehot, preferred_element_type=jnp.float32)
    return chosen.astype(jnp.bfloat16)


def tile_terms(blocks3, subset):
    group_size = math.gcd(subset.shape[0], 8)
    groups = subset.reshape(-1, group_size, 2)

    def group_tiles(group):
        left_block = select_blocks(blocks3, group[:, 0])
        right_block = select_blocks(blocks3, group[:, 1])
        product = jnp.einsum(
            "tsi,tsj->sij", left_block, right_block, preferred_element_type=jnp.float32
        )
        return jnp.where((group[:, 0] >= 0)[:, None, None], product, jnp.float32(0.0))

    return lax.map(group_tiles, groups).reshape(-1, blocks3.shape[2], blocks3.shape[2])


def local_any(slab_grads, query_grads, example_weights, tile_owner):
    tile_table = tile_owner[0]
    tok_count = slab_grads.shape[0]
    slab_full = lax.all_gather(slab_grads, "feat", axis=1, tiled=True)
    blocks3 = slab_full.reshape(tok_count, slab_full.shape[1] // B, B)
    row_total = tok_count * lax.axis_size("ex")
    summed = lax.psum_scatter(
        tile_terms(blocks3, tile_table).astype(jnp.bfloat16), "ex", scatter_dimension=0, tiled=True
    ).astype(jnp.float32)
    gram = (summed / row_total)[None]
    summed = lax.dot_general(
        lax.all_gather(query_grads, "ex", axis=1, tiled=True),
        slab_full,
        (((1,), (1,)), ((), ())),
        preferred_element_type=jnp.float32,
    )
    scores = summed * example_weights[None, :]
    return (gram, scores)


PAIR = ((0, 1), (1, 0), (2, 3), (3, 2))
INNER = ((1, 2), (2, 1))
TO_END = ((1, 0), (2, 3))
TO_MID = ((0, 1), (3, 2))
END_TO_FAR_MID = ((0, 2), (3, 1))
MID_TO_FAR_END = ((1, 3), (2, 0))
CORE = ((0, 1), (1, 0), (2, 3), (3, 2))
ACROSS = ((0, 2), (2, 0), (1, 3), (3, 1))


def tile_call(place, table, always, on_middle=(), on_ends=(), carried=()):
    tiles = table.shape[0]
    lists = [list(always), list(on_middle), list(on_ends)]
    arrays = [x for pairs in lists for pair in pairs for x in pair]
    n = len(arrays)
    wide = arrays[0].shape[1]
    first = sum(pair[0].shape[0] for pair in always)
    total = first + sum(pair[0].shape[0] for pair in on_middle)
    half = tiles // 2
    per = wide // B
    unroll = max(u for u in range(1, 22) if half % u == 0)

    def kernel(place_ref, table_ref, *refs):
        row_refs = refs[:n]
        carried_refs = refs[n : n + len(carried)]
        out_sibling, out_own, rows, turned, sems = refs[n + len(carried) :]
        copies = [[], [], []]
        at = 0
        for which, pairs in enumerate(lists):
            start = 0 if which == 0 else first
            for pair in pairs:
                count = pair[0].shape[0]
                for side in range(2):
                    copies[which].append(
                        pltpu.make_async_copy(
                            row_refs[at], rows.at[side, pl.ds(start, count)], sems.at[at]
                        )
                    )
                    at += 1
                start += count

        def run(some):
            for copy in some:
                copy.start()
            for copy in some:
                copy.wait()

        if on_middle:
            pl.when(place_ref[0] == 1)(lambda: run(copies[1]))
            pl.when(place_ref[0] == 0)(lambda: run(copies[2]))
        run(copies[0])

        for block in range(2 * per):
            side, column = divmod(block * B, wide)
            turned[block] = rows[side, :, column : column + B].T

        def product(tile):
            right = table_ref[tile, 1]
            return jnp.dot(
                turned[table_ref[tile, 0]],
                rows[right // per, :, pl.ds(pl.multiple_of((right % per) * B, B), B)],
                preferred_element_type=jnp.float32,
            )

        def sibling(tile, _):
            out_sibling[tile] = product(tile).astype(out_sibling.dtype)
            return 0

        def mine(tile, _):
            sum_ = product(tile + half)
            for ref in carried_refs:
                sum_ += ref[tile].astype(jnp.float32)
            out_own[tile] = sum_
            return 0

        lax.fori_loop(0, half, sibling, 0, unroll=unroll)
        lax.fori_loop(0, half, mine, 0, unroll=unroll)

    smem = pl.BlockSpec(memory_space=pltpu.SMEM)
    vmem = pl.BlockSpec(memory_space=pltpu.VMEM)
    hbm = pl.BlockSpec(memory_space=pltpu.HBM)
    return pl.pallas_call(
        kernel,
        out_shape=[
            jax.ShapeDtypeStruct((half, B, B), jnp.bfloat16),
            jax.ShapeDtypeStruct((half, B, B), jnp.float32),
        ],
        in_specs=[smem, smem] + [hbm] * n + [vmem] * len(carried),
        out_specs=[vmem, vmem],
        scratch_shapes=[
            pltpu.VMEM((2, total, wide), jnp.bfloat16),
            pltpu.VMEM((2 * per, B, total), jnp.bfloat16),
            pltpu.SemaphoreType.DMA((n,)),
        ],
        compiler_params=pltpu.CompilerParams(vmem_limit_bytes=24 * 2**20),
        cost_estimate=pl.CostEstimate(flops=0, bytes_accessed=0, transcendentals=0),
    )(place, table, *arrays, *carried)


def score_call(place, parts, own, across):
    n, m = len(own), len(parts)
    count = tuple(x.shape[0] for x in own)
    wide = own[0].shape[1]
    quarter = parts[0][0].shape[1]
    lengths = [pair[0].shape[0] for pair in parts]
    group = sum(lengths) // 4
    per = wide // quarter

    def kernel(place_ref, *refs):
        row_refs = refs[: 2 * n]
        query_refs = refs[2 * n : 2 * n + 2 * m]
        outs = refs[2 * n + 2 * m : 3 * n + 2 * m]
        rows, query, sems = refs[3 * n + 2 * m :]

        @pl.when(place_ref[0] == 1)
        def _():
            copies = []
            for i in range(2 * n):
                into = rows.at[i % 2, pl.ds(sum(count[: i // 2]), count[i // 2])]
                copies.append(pltpu.make_async_copy(row_refs[i], into, sems.at[i]))
            for i in range(2 * m):
                into = query.at[i % 2, pl.ds(sum(lengths[: i // 2]), lengths[i // 2])]
                copies.append(pltpu.make_async_copy(query_refs[i], into, sems.at[2 * n + i]))
            for copy in copies:
                copy.start()
            for copy in copies:
                copy.wait()
            for i in range(n):
                for j in range(2):
                    total = None
                    for k in range(4):
                        spot = place_ref[1 + k]
                        term = lax.dot_general(
                            query[j, k * group : (k + 1) * group, :],
                            rows[
                                spot // per,
                                sum(count[:i]) : sum(count[: i + 1]),
                                pl.ds(pl.multiple_of((spot % per) * quarter, quarter), quarter),
                            ],
                            (((1,), (1,)), ((), ())),
                            preferred_element_type=jnp.float32,
                        )
                        total = term if total is None else total + term
                    outs[i][j] = total.astype(outs[i].dtype)

    smem = pl.BlockSpec(memory_space=pltpu.SMEM)
    hbm = pl.BlockSpec(memory_space=pltpu.HBM)
    vmem = pl.BlockSpec(memory_space=pltpu.VMEM)
    arrays = [x for pair in zip(own, across) for x in pair] + [x for pair in parts for x in pair]
    return pl.pallas_call(
        kernel,
        out_shape=[jax.ShapeDtypeStruct((2, group, c), jnp.bfloat16) for c in count],
        in_specs=[smem] + [hbm] * len(arrays),
        out_specs=[vmem] * n,
        scratch_shapes=[
            pltpu.VMEM((2, sum(count), wide), jnp.bfloat16),
            pltpu.VMEM((2, 4 * group, quarter), jnp.bfloat16),
            pltpu.SemaphoreType.DMA((len(arrays),)),
        ],
        compiler_params=pltpu.CompilerParams(vmem_limit_bytes=24 * 2**20),
        cost_estimate=pl.CostEstimate(flops=0, bytes_accessed=0, transcendentals=0),
    )(place, *arrays)


def after(values, *done):
    return lax.optimization_barrier(tuple(values) + done)[: len(values)]


def local_line(slab_grads, query_grads, example_weights, tile_owner):
    count, quarter = slab_grads.shape
    half, piece = count // 2, count // 4
    e = lax.axis_index("ex")
    f = lax.axis_index("feat")
    core = f % 2
    middle = jnp.logical_or(e == 1, e == 2)
    late = (e >= 2).astype(jnp.int32)

    def move(value, pairs):
        return lax.ppermute(value, "ex", pairs)

    def across(value):
        return lax.ppermute(value, "feat", ACROSS)

    def across_on(value, which):
        pairs = [(p * 4 + g, p * 4 + (g ^ 2)) for p in which for g in range(4)]
        return lax.ppermute(value, ("ex", "feat"), pairs)

    def join(*values):
        return jnp.concatenate(values, axis=0)

    def cores(value):
        pairs = [(p * 4 + g, p * 4 + (g ^ 1)) for p in (1, 2) for g in range(4)]
        return lax.ppermute(value, ("ex", "feat"), pairs)

    slots = tile_owner.shape[1] // 4
    own_tiles = lax.dynamic_slice(tile_owner[0], (e * slots, 0), (slots, 2))
    tiles = jnp.concatenate([lax.ppermute(own_tiles, "feat", CORE), own_tiles], axis=0)
    blocks = quarter // B
    tiles = jnp.maximum(tiles, 0)
    table = ((tiles // blocks) ^ f) * blocks + tiles % blocks
    order = jnp.where(e == 2, jnp.array([2, 3, 1, 0]), jnp.array([1, 0, 2, 3])).astype(jnp.int32)
    place = jnp.concatenate([middle.astype(jnp.int32)[None], order ^ f])

    keep = lax.dynamic_slice(slab_grads, (core * half, 0), (half, quarter))
    give = lax.dynamic_slice(slab_grads, ((1 - core) * half, 0), (half, quarter))
    own = jnp.concatenate([keep, lax.ppermute(give, "feat", CORE)], axis=1)

    own_x = across(own)
    near = move(own, PAIR)
    inner = move(own, INNER)

    near, inner, query_grads, table = after((near, inner, query_grads, table), own_x)
    near_x = across(near)
    outer = move(near, INNER)
    inner_end = move(inner, TO_END)
    q_end = move(query_grads, TO_MID)
    q_half = query_grads.shape[0] // 2
    mine = lax.dynamic_slice(query_grads, (late * q_half, 0), (q_half, quarter))
    other = lax.dynamic_slice(query_grads, ((1 - late) * q_half, 0), (q_half, quarter))

    inner, inner_end, outer, near, near_x = after((inner, inner_end, outer, near, near_x))
    second = jnp.where(middle, inner, inner_end)
    second_x = across(second)
    outer_end0 = move(outer[:piece], TO_END)
    outer_end1 = move(outer[piece:], TO_END)
    outer_x = across_on(outer, (1, 2))

    q_end, near, mine = after((q_end, near, mine), second)
    end_mine = lax.dynamic_slice(q_end, (late * q_half, 0), (q_half, quarter))
    end_other = lax.dynamic_slice(q_end, ((1 - late) * q_half, 0), (q_half, quarter))
    q_inner = move(join(other, end_other), INNER)
    sibling1, sum1 = tile_call(place, table, [(own, own_x), (near, near_x)])

    outer_end0, outer_end1, end_mine, mine, sibling1 = after(
        (outer_end0, outer_end1, end_mine, mine, sibling1), sum1
    )
    outer_end_x0 = across_on(outer_end0, (0, 3))
    outer_end_x1 = across_on(outer_end1, (0, 3))

    mine, end_mine, q_inner, sibling1 = after((mine, end_mine, q_inner, sibling1), outer_end1)
    sibling1 = lax.ppermute(sibling1, "feat", CORE)
    parts = [(mine, cores(mine)), (end_mine, cores(end_mine)), (q_inner, cores(q_inner))]

    own, second = after((own, second), second_x, outer_end_x0)
    r_own, r_near, r_inner = score_call(place, parts, [own, near, second], [own_x, near_x, second_x])
    to_end = move(r_near, TO_END)
    to_mid = move(r_inner, INNER)
    second, second_x = after((second, second_x), r_own)
    sibling2, sum2 = tile_call(place, table, [(second, second_x)], carried=[sum1, sibling1])
    sibling2 = lax.ppermute(sibling2, "feat", CORE)

    outer, outer_x = after((outer, outer_x), sum2)
    (r_outer,) = score_call(place, parts, [outer], [outer_x])
    to_far = move(r_outer, MID_TO_FAR_END)
    outer, outer_x = after((outer, outer_x), r_outer)
    sibling3, sum3 = tile_call(
        place,
        table,
        [],
        [(outer, outer_x)],
        [(outer_end0, outer_end_x0), (outer_end1, outer_end_x1)],
        [sum2],
    )
    sibling3 = lax.ppermute(sibling3, "feat", CORE)
    gram = sum3 + sibling2.astype(jnp.float32) + sibling3.astype(jnp.float32)
    gram = gram / (count * 4)
    gram = jnp.where((own_tiles[:, 0] >= 0)[:, None, None], gram, jnp.float32(0.0))

    first = jnp.where(middle, r_own, to_end)
    rest = jnp.where(middle, to_mid, to_far)
    low = jnp.where(late == 1, rest, first)
    high = jnp.where(late == 1, first, rest)
    both = jnp.concatenate([low, high], axis=1)
    got = lax.ppermute(both[1], "feat", CORE)
    left = jnp.where(core == 0, both[0], got)
    right = jnp.where(core == 0, got, both[0])
    scores = jnp.concatenate([left, right], axis=1).astype(jnp.float32)
    return gram[None], scores * example_weights[None, :]


def solution(mesh):
    placed = (
        P(("grp", "ex"), "feat"),
        P(("grp", "feat"), "ex"),
        P(("grp", "ex")),
        P(("grp", "feat"), None, None),
    )

    line = mesh.shape["ex"] == 4 and mesh.shape["feat"] == 4
    return jax.shard_map(
        local_line if line else local_any,
        mesh=mesh,
        in_specs=placed,
        out_specs=(P(("grp", "feat"), "ex", None, None), P(("grp", "feat"), "ex")),
        check_vma=False,
    )
```

```python
import math

import jax
import jax.numpy as jnp
from jax import lax
from jax.experimental import pallas as pl
from jax.experimental.pallas import tpu as pltpu
from jax.sharding import PartitionSpec as P

B = 128


def select_blocks(blocks3, indices):
    block_ids = lax.broadcasted_iota(jnp.int32, (indices.shape[0], blocks3.shape[1]), 1)
    onehot = (indices[:, None] == block_ids).astype(jnp.bfloat16)
    chosen = jnp.einsum("tnb,gn->tgb", blocks3, onehot, preferred_element_type=jnp.float32)
    return chosen.astype(jnp.bfloat16)


def tile_terms(blocks3, subset):
    group_size = math.gcd(subset.shape[0], 8)
    groups = subset.reshape(-1, group_size, 2)

    def group_tiles(group):
        left_block = select_blocks(blocks3, group[:, 0])
        right_block = select_blocks(blocks3, group[:, 1])
        product = jnp.einsum(
            "tsi,tsj->sij", left_block, right_block, preferred_element_type=jnp.float32
        )
        return jnp.where((group[:, 0] >= 0)[:, None, None], product, jnp.float32(0.0))

    return lax.map(group_tiles, groups).reshape(-1, blocks3.shape[2], blocks3.shape[2])


def local_any(slab_grads, query_grads, example_weights, tile_owner):
    tile_table = tile_owner[0]
    tok_count = slab_grads.shape[0]
    slab_full = lax.all_gather(slab_grads, "feat", axis=1, tiled=True)
    blocks3 = slab_full.reshape(tok_count, slab_full.shape[1] // B, B)
    row_total = tok_count * lax.axis_size("ex")
    summed = lax.psum_scatter(
        tile_terms(blocks3, tile_table).astype(jnp.bfloat16), "ex", scatter_dimension=0, tiled=True
    ).astype(jnp.float32)
    gram = (summed / row_total)[None]
    summed = lax.dot_general(
        lax.all_gather(query_grads, "ex", axis=1, tiled=True),
        slab_full,
        (((1,), (1,)), ((), ())),
        preferred_element_type=jnp.float32,
    )
    scores = summed * example_weights[None, :]
    return (gram, scores)


PAIR = ((0, 1), (1, 0), (2, 3), (3, 2))
INNER = ((1, 2), (2, 1))
TO_END = ((1, 0), (2, 3))
TO_MID = ((0, 1), (3, 2))
END_TO_FAR_MID = ((0, 2), (3, 1))
MID_TO_FAR_END = ((1, 3), (2, 0))
CORE = ((0, 1), (1, 0), (2, 3), (3, 2))
ACROSS = ((0, 2), (2, 0), (1, 3), (3, 1))


def plan(batches, own_count):
    out = []
    for sides in batches:
        for side in range(2):
            at = own_count
            for given, start, count, *flip in sides[side]:
                for plane, array in zip((1, 0), given) if isinstance(given, tuple) else [(2, given)]:
                    wide = array.shape[1]
                    if any(flip):
                        out.append((array, start, count, side, at, 0, wide // 2, wide // 2, plane))
                        out.append((array, start, count, side, at, wide // 2, 0, wide // 2, plane))
                    else:
                        out.append((array, start, count, side, at, 0, 0, wide, plane))
                at += count
    return out


def rows_of(batches):
    return sum(entry[2] for sides in batches[:1] for entry in sides[0])


def tile_call(place, table, always, carried=(), carried_sibling=None, part="both", scores=None):
    tiles = table.shape[0]
    moves = [plan([always], 0)]
    arrays = []
    for some in moves:
        for array, *_ in some:
            if not any(array is x for x in arrays):
                arrays.append(array)
    where = [[next(i for i, x in enumerate(arrays) if x is m[0]) for m in some] for some in moves]
    n = len(arrays)
    n_moves = sum(len(some) for some in moves)
    wide = arrays[0].shape[1]
    total = rows_of([always])
    half = tiles // 2
    per = wide // B
    extra = [] if carried_sibling is None else [carried_sibling]
    carried = list(carried) + extra
    n_own = len(carried) - len(extra)
    unroll = max(u for u in range(1, 22) if half // 2 % u == 0)
    n_out = 2 if part == "both" else 1

    n_scores = len(scores.count) if scores else 0
    score_arrays = scores.arrays if scores else []
    n_in = n + len(carried) + len(score_arrays)

    def kernel(place_ref, table_ref, *refs):
        score_sources = refs[n + len(carried) : n_in]
        score_outs = refs[n_in + n_out : n_in + n_out + n_scores]
        refs = refs[: n + len(carried)] + refs[n_in : n_in + n_out] + refs[n_in + n_out + n_scores :]
        if scores:
            score_scratch, refs = refs[-3:], refs[:-3]
            score_copies = scores.copies(score_sources, *score_scratch)
        row_refs = refs[:n]
        carried_refs = refs[n : n + len(carried)]
        out_refs = refs[n + len(carried) : n + len(carried) + n_out]
        outs = refs[n + len(carried) + n_out : -3 - len(carried)]
        held = refs[-3 - len(carried) : -3]
        rows, turned, sems = refs[-3:]
        held_copies = [
            pltpu.make_async_copy(ref, held[i], sems.at[n_moves + i])
            for i, ref in enumerate(carried_refs)
        ]
        parts = []
        for i in range(n_out):
            for j in range(2):
                some = pl.ds(j * (half // 2), half // 2)
                sem = sems.at[n_moves + len(carried) + 2 * i + j]
                parts.append(pltpu.make_async_copy(outs[i].at[some], out_refs[i].at[some], sem))
        copies = [[], [], []]
        at = 0
        for i, some in enumerate(moves):
            for (_, start, count, side, to, left, right, columns, plane), index in zip(some, where[i]):
                source = row_refs[index].at[pl.ds(start, count), pl.ds(left, columns)]
                into = rows.at[side, pl.ds(to, count), pl.ds(right, columns)]
                copies[plane].append(pltpu.make_async_copy(source, into, sems.at[at]))
                at += 1

        def each(some, do):
            for copy in some:
                do(copy)

        def rows_do(do):
            each(copies[2], do)
            for plane in range(2):
                if copies[plane]:
                    pl.when(place_ref[0] == plane)(lambda plane=plane: each(copies[plane], do))

        rows_do(lambda copy: copy.start())
        each(held_copies, lambda copy: copy.start())
        if scores:
            pl.when(place_ref[0] == 1)(lambda: each(score_copies, lambda copy: copy.start()))
        rows_do(lambda copy: copy.wait())

        for block in range(2 * per):
            side, column = divmod(block * B, wide)
            turned[block] = rows[side, :, column : column + B].T

        def product(tile):
            right = table_ref[tile, 1]
            return jnp.dot(
                turned[table_ref[tile, 0]],
                rows[right // per, :, pl.ds(pl.multiple_of((right % per) * B, B), B)],
                preferred_element_type=jnp.float32,
            )

        def sibling(tile, _):
            sum_ = product(tile)
            for ref in held[n_own:]:
                sum_ += ref[tile].astype(jnp.float32)
            outs[0][tile] = sum_.astype(outs[0].dtype)
            return 0

        def mine(tile, _):
            sum_ = product(tile + half)
            for ref in held[:n_own]:
                sum_ += ref[tile].astype(jnp.float32)
            if part == "own":
                scale = 1.0 / place_ref[7].astype(jnp.float32)
                sum_ = sum_ * jnp.where(table_ref[tile + half, 2] == 1, scale, 0.0)
            outs[-1][tile] = sum_
            return 0

        if part != "own":
            for copy in held_copies[n_own:]:
                copy.wait()
            for j in range(2):
                lax.fori_loop(j * (half // 2), (j + 1) * (half // 2), sibling, 0, unroll=unroll)
                parts[j].start()
        if part != "sibling":
            for copy in held_copies[:n_own]:
                copy.wait()
            for j in range(2):
                lax.fori_loop(j * (half // 2), (j + 1) * (half // 2), mine, 0, unroll=unroll)
                parts[j - 2].start()
        if scores:

            @pl.when(place_ref[0] == 1)
            def _():
                scores.compute(place_ref, score_outs, *score_scratch[:2], score_copies)

        for copy in parts:
            copy.wait()

    smem = pl.BlockSpec(memory_space=pltpu.SMEM)
    hbm = pl.BlockSpec(memory_space=pltpu.HBM)
    outs = []
    if part != "own":
        outs.append(jax.ShapeDtypeStruct((half, B, B), jnp.bfloat16))
    if part != "sibling":
        outs.append(jax.ShapeDtypeStruct((half, B, B), jnp.float32))
    return pl.pallas_call(
        kernel,
        out_shape=outs + (scores.out_shape if scores else []),
        in_specs=[smem, smem] + [hbm] * n_in,
        out_specs=[hbm] * n_out + [pl.BlockSpec(memory_space=pltpu.VMEM)] * n_scores,
        scratch_shapes=[pltpu.VMEM(x.shape, x.dtype) for x in outs + list(carried)]
        + [
            pltpu.VMEM((2, total, wide), jnp.bfloat16),
            pltpu.VMEM((2 * per, B, total), jnp.bfloat16),
            pltpu.SemaphoreType.DMA((n_moves + len(carried) + 2 * n_out,)),
        ]
        + (scores.scratch if scores else []),
        compiler_params=pltpu.CompilerParams(vmem_limit_bytes=18 * 2**20),
        cost_estimate=pl.CostEstimate(flops=0, bytes_accessed=0, transcendentals=0),
    )(place, table, *arrays, *carried, *score_arrays)


class Scores:
    def __init__(self, parts, slots):
        self.count = [rows_of([slot]) for slot in slots]
        self.moves = []
        for i, slot in enumerate(slots):
            self.moves += plan([slot], sum(self.count[:i]))
        self.quarter = parts[0][0].shape[1]
        lengths = [pair[0].shape[0] for pair in parts]
        for i, pair in enumerate(parts):
            for j in range(2):
                at = sum(lengths[:i])
                self.moves.append((pair[j], 0, lengths[i], 2 + j, at, 0, 0, self.quarter, 2))
        self.wide = self.moves[0][0].shape[1]
        self.group = sum(lengths) // 4
        self.arrays = [move[0] for move in self.moves]
        self.out_shape = [
            jax.ShapeDtypeStruct((2, self.group, c), jnp.bfloat16) for c in self.count
        ]
        self.scratch = [
            pltpu.VMEM((2, sum(self.count), self.wide), jnp.bfloat16),
            pltpu.VMEM((2, 4 * self.group, self.quarter), jnp.bfloat16),
            pltpu.SemaphoreType.DMA((len(self.moves),)),
        ]

    def copies(self, sources, rows, query, sems):
        out = []
        for i, (_, start, count, side, to, *_) in enumerate(self.moves):
            into = rows.at[side, pl.ds(to, count)] if side < 2 else query.at[side - 2, pl.ds(to, count)]
            out.append(pltpu.make_async_copy(sources[i].at[pl.ds(start, count)], into, sems.at[i]))
        return out

    def compute(self, place_ref, outs, rows, query, copies):
        group, quarter = self.group, self.quarter
        per = self.wide // quarter
        for copy, move in zip(copies, self.moves):
            if move[3] >= 2:
                copy.wait()
        for i, out in enumerate(outs):
            first = sum(self.count[:i])
            for copy, move in zip(copies, self.moves):
                if move[3] < 2 and first <= move[4] < first + self.count[i]:
                    copy.wait()
            for j in range(2):
                total = None
                for k in range(4):
                    spot = place_ref[1 + k]
                    columns = pl.ds(pl.multiple_of((spot % per) * quarter, quarter), quarter)
                    term = lax.dot_general(
                        query[j, k * group : (k + 1) * group, :],
                        rows[spot // per, first : first + self.count[i], columns],
                        (((1,), (1,)), ((), ())),
                        preferred_element_type=jnp.float32,
                    )
                    total = term if total is None else total + term
                out[j] = total.astype(out.dtype)


def score_call(place, parts, slots):
    scores = Scores(parts, slots)
    n, m = len(slots), len(scores.moves)

    def kernel(place_ref, *refs):
        outs = refs[m : m + n]
        rows, query, sems = refs[m + n :]

        @pl.when(place_ref[0] == 1)
        def _():
            copies = scores.copies(refs[:m], rows, query, sems)
            for copy, move in zip(copies, scores.moves):
                if move[3] >= 2:
                    copy.start()
            for copy, move in zip(copies, scores.moves):
                if move[3] < 2:
                    copy.start()
            scores.compute(place_ref, outs, rows, query, copies)

    smem = pl.BlockSpec(memory_space=pltpu.SMEM)
    hbm = pl.BlockSpec(memory_space=pltpu.HBM)
    vmem = pl.BlockSpec(memory_space=pltpu.VMEM)
    return pl.pallas_call(
        kernel,
        out_shape=scores.out_shape,
        in_specs=[smem] + [hbm] * m,
        out_specs=[vmem] * n,
        scratch_shapes=scores.scratch,
        compiler_params=pltpu.CompilerParams(vmem_limit_bytes=18 * 2**20),
        cost_estimate=pl.CostEstimate(flops=0, bytes_accessed=0, transcendentals=0),
    )(place, *scores.arrays)


def weigh_call(place, on_middle, on_ends, swapped, weights):
    group, count = swapped[0].shape

    def kernel(place_ref, *refs):
        late, core = place_ref[5], place_ref[6]
        weight, out = refs[6], refs[7]

        def put(i, block, own_rows):
            row = late if i == 0 else 1 - late
            column = core if own_rows else 1 - core
            across = pl.ds(pl.multiple_of(column * count, count), count)
            down = pl.ds(pl.multiple_of(row * group, group), group)
            out[down, across] = block.astype(jnp.float32) * weight[:, across]

        for i in range(2):
            pl.when(place_ref[0] == 1)(lambda i=i: put(i, refs[i][0], True))
            pl.when(place_ref[0] == 0)(lambda i=i: put(i, refs[2 + i][0], True))
            put(i, refs[4 + i][...], False)

    smem = pl.BlockSpec(memory_space=pltpu.SMEM)
    vmem = pl.BlockSpec(memory_space=pltpu.VMEM)
    return pl.pallas_call(
        kernel,
        out_shape=jax.ShapeDtypeStruct((2 * group, 2 * count), jnp.float32),
        in_specs=[smem] + [vmem] * 7,
        out_specs=vmem,
        cost_estimate=pl.CostEstimate(flops=0, bytes_accessed=0, transcendentals=0),
    )(place, *on_middle, *on_ends, *swapped, weights)


def after(values, *done):
    return lax.optimization_barrier(tuple(values) + done)[: len(values)]


def local_line(slab_grads, query_grads, example_weights, tile_owner):
    count, quarter = slab_grads.shape
    half, piece = count // 2, count // 4
    e = lax.axis_index("ex")
    f = lax.axis_index("feat")
    core = f % 2
    middle = jnp.logical_or(e == 1, e == 2)
    late = (e >= 2).astype(jnp.int32)

    def move(value, pairs):
        return lax.ppermute(value, "ex", pairs)

    def across(value):
        return lax.ppermute(value, "feat", ACROSS)

    def swap(value):
        return lax.ppermute(value, "feat", CORE)

    def across_on(value, which):
        pairs = [(p * 4 + g, p * 4 + (g ^ 2)) for p in which for g in range(4)]
        return lax.ppermute(value, ("ex", "feat"), pairs)

    def swap_on(value, which):
        pairs = [(p * 4 + g, p * 4 + (g ^ 1)) for p in which for g in range(4)]
        return lax.ppermute(value, ("ex", "feat"), pairs)

    mids, ends = (1, 2), (0, 3)

    def whole(a, b):
        return ([(a, 0, half)], [(b, 0, half)])

    slots = tile_owner.shape[1] // 4
    own_tiles = lax.dynamic_slice(tile_owner[0], (e * slots, 0), (slots, 2))
    tiles = jnp.concatenate([swap(own_tiles), own_tiles], axis=0)
    blocks = quarter // B
    valid = (tiles[:, :1] >= 0).astype(jnp.int32)
    tiles = jnp.maximum(tiles, 0)
    table = ((tiles // blocks) ^ f) * blocks + tiles % blocks
    table = jnp.concatenate([table, valid], axis=1)
    order = jnp.where(e == 2, jnp.array([2, 3, 1, 0]), jnp.array([1, 0, 2, 3])).astype(jnp.int32)
    place = jnp.concatenate(
        [
            middle.astype(jnp.int32)[None],
            order ^ f,
            late[None],
            core[None],
            jnp.array([4 * count], jnp.int32),
        ]
    )

    keep = lax.dynamic_slice(slab_grads, (core * half, 0), (half, quarter))
    give = lax.dynamic_slice(slab_grads, ((1 - core) * half, 0), (half, quarter))
    own = jnp.concatenate([keep, swap(give)], axis=1)
    q_half = query_grads.shape[0] // 2

    own_x = across(own)
    near = move(own, PAIR)
    inner = move(own, INNER)

    def halves(value, which):
        return lax.dynamic_slice(value, (which * q_half, 0), (q_half, quarter))

    q_mine, q_other = halves(query_grads, late), halves(query_grads, 1 - late)
    near, inner, own, own_x, q_mine, q_other, table = after(
        (near, inner, own, own_x, q_mine, q_other, table)
    )
    near_x = across(near)
    outer = move(near, INNER)
    inner_end = move(inner, TO_END)
    q_end_other = move(q_other, TO_MID)
    q_mine_sibling = swap(q_mine)
    sibling0, sum0 = tile_call(place, table, whole(own, own_x))

    inner, inner_end, outer, near, near_x, q_end_other, q_mine, sibling0, sum0 = after(
        (inner, inner_end, outer, near, near_x, q_end_other, q_mine, sibling0, sum0)
    )
    second = jnp.where(middle, outer, inner_end)
    second_x = across(second)
    outer_end = move(outer, TO_END)
    q_inner = move(q_other, INNER)
    q_far = move(q_end_other, INNER)
    q_end = move(q_mine, TO_MID)
    sibling1, sum1 = tile_call(place, table, whole(near, near_x), [sum0], sibling0)

    second, second_x, outer_end, inner, sum1, sibling1 = after(
        (second, second_x, outer_end, inner, sum1, sibling1)
    )
    third = jnp.where(middle, inner, outer_end)
    third_x = across(third)
    parts = [(q_mine, q_mine_sibling)] + [(x, swap(x)) for x in (q_end, q_inner, q_far)]
    slots3 = [whole(own, own_x), whole(near, near_x), whole(second, second_x)]
    r_own, r_near, r_outer = score_call(place, parts, slots3)
    to_far = move(r_outer, MID_TO_FAR_END)
    to_end = move(r_near, TO_END)
    sibling2, sum2 = tile_call(place, table, whole(second, second_x), [sum1], sibling1)
    third_sibling = swap(third)

    third_x, to_end, sibling2 = after((third_x, to_end, sibling2), sum2, r_own)
    third_x_sibling = swap(third_x)
    (r_inner,) = score_call(place, parts, [whole(third, third_x)])
    sibling2 = swap(sibling2)
    sibling2, r_inner, third_x_sibling = after((sibling2, r_inner, third_x_sibling))
    to_mid = move(r_inner, INNER)
    (gram,) = tile_call(
        place,
        table,
        (
            [(third, 0, half), (third_sibling, 0, half, True)],
            [(third_x, 0, half), (third_x_sibling, 0, half, True)],
        ),
        [sum2, sibling2],
        part="own",
    )
    to_end, to_far, to_mid, gram = after((to_end, to_far, to_mid, gram))
    first_sibling = swap(jnp.where(middle, r_own[1], to_end[1]))
    rest_sibling = swap(jnp.where(middle, to_mid[1], to_far[1]))
    scores = weigh_call(
        place,
        (r_own, to_mid),
        (to_end, to_far),
        (first_sibling, rest_sibling),
        example_weights[None, :],
    )
    return gram[None], scores


def solution(mesh):
    placed = (
        P(("grp", "ex"), "feat"),
        P(("grp", "feat"), "ex"),
        P(("grp", "ex")),
        P(("grp", "feat"), None, None),
    )

    line = mesh.shape["ex"] == 4 and mesh.shape["feat"] == 4
    return jax.shard_map(
        local_line if line else local_any,
        mesh=mesh,
        in_specs=placed,
        out_specs=(P(("grp", "feat"), "ex", None, None), P(("grp", "feat"), "ex")),
        check_vma=False,
    )
```

```python
import math

import jax
import jax.numpy as jnp
from jax import lax
from jax.experimental import pallas as pl
from jax.experimental.pallas import tpu as pltpu
from jax.sharding import PartitionSpec as P

B = 128


def select_blocks(blocks3, indices):
    block_ids = lax.broadcasted_iota(jnp.int32, (indices.shape[0], blocks3.shape[1]), 1)
    onehot = (indices[:, None] == block_ids).astype(jnp.bfloat16)
    chosen = jnp.einsum("tnb,gn->tgb", blocks3, onehot, preferred_element_type=jnp.float32)
    return chosen.astype(jnp.bfloat16)


def tile_terms(blocks3, subset):
    group_size = math.gcd(subset.shape[0], 8)
    groups = subset.reshape(-1, group_size, 2)

    def group_tiles(group):
        left_block = select_blocks(blocks3, group[:, 0])
        right_block = select_blocks(blocks3, group[:, 1])
        product = jnp.einsum(
            "tsi,tsj->sij", left_block, right_block, preferred_element_type=jnp.float32
        )
        return jnp.where((group[:, 0] >= 0)[:, None, None], product, jnp.float32(0.0))

    return lax.map(group_tiles, groups).reshape(-1, blocks3.shape[2], blocks3.shape[2])


def local_any(slab_grads, query_grads, example_weights, tile_owner):
    tile_table = tile_owner[0]
    tok_count = slab_grads.shape[0]
    slab_full = lax.all_gather(slab_grads, "feat", axis=1, tiled=True)
    blocks3 = slab_full.reshape(tok_count, slab_full.shape[1] // B, B)
    row_total = tok_count * lax.axis_size("ex")
    summed = lax.psum_scatter(
        tile_terms(blocks3, tile_table).astype(jnp.bfloat16), "ex", scatter_dimension=0, tiled=True
    ).astype(jnp.float32)
    gram = (summed / row_total)[None]
    summed = lax.dot_general(
        lax.all_gather(query_grads, "ex", axis=1, tiled=True),
        slab_full,
        (((1,), (1,)), ((), ())),
        preferred_element_type=jnp.float32,
    )
    scores = summed * example_weights[None, :]
    return (gram, scores)


PAIR = ((0, 1), (1, 0), (2, 3), (3, 2))
INNER = ((1, 2), (2, 1))
TO_END = ((1, 0), (2, 3))
TO_MID = ((0, 1), (3, 2))
END_TO_FAR_MID = ((0, 2), (3, 1))
MID_TO_FAR_END = ((1, 3), (2, 0))
CORE = ((0, 1), (1, 0), (2, 3), (3, 2))
ACROSS = ((0, 2), (2, 0), (1, 3), (3, 1))


def plan(batches, own_count):
    out = []
    for sides in batches:
        for side in range(2):
            at = own_count
            for given, start, count, *flip in sides[side]:
                for plane, array in zip((1, 0), given) if isinstance(given, tuple) else [(2, given)]:
                    wide = array.shape[1]
                    if any(flip):
                        out.append((array, start, count, side, at, 0, wide // 2, wide // 2, plane))
                        out.append((array, start, count, side, at, wide // 2, 0, wide // 2, plane))
                    else:
                        out.append((array, start, count, side, at, 0, 0, wide, plane))
                at += count
    return out


def rows_of(batches):
    return sum(entry[2] for sides in batches[:1] for entry in sides[0])


def tile_call(place, table, always, carried=(), carried_sibling=None, part="both", scores=None):
    tiles = table.shape[0]
    moves = [plan([always], 0)]
    arrays = []
    for some in moves:
        for array, *_ in some:
            if not any(array is x for x in arrays):
                arrays.append(array)
    where = [[next(i for i, x in enumerate(arrays) if x is m[0]) for m in some] for some in moves]
    n = len(arrays)
    n_moves = sum(len(some) for some in moves)
    wide = arrays[0].shape[1]
    total = rows_of([always])
    half = tiles // 2
    per = wide // B
    extra = [] if carried_sibling is None else [carried_sibling]
    carried = list(carried) + extra
    n_own = len(carried) - len(extra)
    unroll = max(u for u in range(1, 22) if half // 2 % u == 0)
    n_out = 2 if part == "both" else 1

    n_scores = len(scores.count) if scores else 0
    score_arrays = scores.arrays if scores else []
    n_in = n + len(carried) + len(score_arrays)

    def kernel(place_ref, table_ref, *refs):
        score_sources = refs[n + len(carried) : n_in]
        score_outs = refs[n_in + n_out : n_in + n_out + n_scores]
        refs = refs[: n + len(carried)] + refs[n_in : n_in + n_out] + refs[n_in + n_out + n_scores :]
        if scores:
            score_scratch, refs = refs[-3:], refs[:-3]
            score_copies = scores.copies(score_sources, *score_scratch)
        row_refs = refs[:n]
        carried_refs = refs[n : n + len(carried)]
        out_refs = refs[n + len(carried) : n + len(carried) + n_out]
        outs = refs[n + len(carried) + n_out : -3 - len(carried)]
        held = refs[-3 - len(carried) : -3]
        rows, turned, sems = refs[-3:]
        held_copies = [
            pltpu.make_async_copy(ref, held[i], sems.at[n_moves + i])
            for i, ref in enumerate(carried_refs)
        ]
        parts = []
        for i in range(n_out):
            for j in range(2):
                some = pl.ds(j * (half // 2), half // 2)
                sem = sems.at[n_moves + len(carried) + 2 * i + j]
                parts.append(pltpu.make_async_copy(outs[i].at[some], out_refs[i].at[some], sem))
        copies = [[], [], []]
        at = 0
        for i, some in enumerate(moves):
            for (_, start, count, side, to, left, right, columns, plane), index in zip(some, where[i]):
                source = row_refs[index].at[pl.ds(start, count), pl.ds(left, columns)]
                into = rows.at[side, pl.ds(to, count), pl.ds(right, columns)]
                copies[plane].append(pltpu.make_async_copy(source, into, sems.at[at]))
                at += 1

        def each(some, do):
            for copy in some:
                do(copy)

        def rows_do(do):
            each(copies[2], do)
            for plane in range(2):
                if copies[plane]:
                    pl.when(place_ref[0] == plane)(lambda plane=plane: each(copies[plane], do))

        rows_do(lambda copy: copy.start())
        each(held_copies, lambda copy: copy.start())
        if scores:
            pl.when(place_ref[0] == 1)(lambda: each(score_copies, lambda copy: copy.start()))
        rows_do(lambda copy: copy.wait())

        for block in range(2 * per):
            side, column = divmod(block * B, wide)
            turned[block] = rows[side, :, column : column + B].T

        def product(tile):
            right = table_ref[tile, 1]
            return jnp.dot(
                turned[table_ref[tile, 0]],
                rows[right // per, :, pl.ds(pl.multiple_of((right % per) * B, B), B)],
                preferred_element_type=jnp.float32,
            )

        def sibling(tile, _):
            sum_ = product(tile)
            for ref in held[n_own:]:
                sum_ += ref[tile].astype(jnp.float32)
            outs[0][tile] = sum_.astype(outs[0].dtype)
            return 0

        def mine(tile, _):
            sum_ = product(tile + half)
            for ref in held[:n_own]:
                sum_ += ref[tile].astype(jnp.float32)
            if part == "own":
                scale = 1.0 / place_ref[7].astype(jnp.float32)
                sum_ = sum_ * jnp.where(table_ref[tile + half, 2] == 1, scale, 0.0)
            outs[-1][tile] = sum_
            return 0

        if part != "own":
            for copy in held_copies[n_own:]:
                copy.wait()
            for j in range(2):
                lax.fori_loop(j * (half // 2), (j + 1) * (half // 2), sibling, 0, unroll=unroll)
                parts[j].start()
        if part != "sibling":
            for copy in held_copies[:n_own]:
                copy.wait()
            for j in range(2):
                lax.fori_loop(j * (half // 2), (j + 1) * (half // 2), mine, 0, unroll=unroll)
                parts[j - 2].start()
        if scores:

            @pl.when(place_ref[0] == 1)
            def _():
                scores.compute(place_ref, score_outs, *score_scratch[:2], score_copies)

        for copy in parts:
            copy.wait()

    smem = pl.BlockSpec(memory_space=pltpu.SMEM)
    hbm = pl.BlockSpec(memory_space=pltpu.HBM)
    outs = []
    if part != "own":
        outs.append(jax.ShapeDtypeStruct((half, B, B), jnp.bfloat16))
    if part != "sibling":
        outs.append(jax.ShapeDtypeStruct((half, B, B), jnp.float32))
    return pl.pallas_call(
        kernel,
        out_shape=outs + (scores.out_shape if scores else []),
        in_specs=[smem, smem] + [hbm] * n_in,
        out_specs=[hbm] * n_out + [pl.BlockSpec(memory_space=pltpu.VMEM)] * n_scores,
        scratch_shapes=[pltpu.VMEM(x.shape, x.dtype) for x in outs + list(carried)]
        + [
            pltpu.VMEM((2, total, wide), jnp.bfloat16),
            pltpu.VMEM((2 * per, B, total), jnp.bfloat16),
            pltpu.SemaphoreType.DMA((n_moves + len(carried) + 2 * n_out,)),
        ]
        + (scores.scratch if scores else []),
        compiler_params=pltpu.CompilerParams(vmem_limit_bytes=18 * 2**20),
        cost_estimate=pl.CostEstimate(flops=0, bytes_accessed=0, transcendentals=0),
    )(place, table, *arrays, *carried, *score_arrays)


class Scores:
    def __init__(self, parts, slots):
        self.count = [rows_of([slot]) for slot in slots]
        self.moves = []
        for i, slot in enumerate(slots):
            self.moves += plan([slot], sum(self.count[:i]))
        self.quarter = parts[0][0].shape[1]
        lengths = [pair[0].shape[0] for pair in parts]
        for i, pair in enumerate(parts):
            for j in range(2):
                at = sum(lengths[:i])
                self.moves.append((pair[j], 0, lengths[i], 2 + j, at, 0, 0, self.quarter, 2))
        self.wide = self.moves[0][0].shape[1]
        self.group = sum(lengths) // 4
        self.arrays = [move[0] for move in self.moves]
        self.out_shape = [
            jax.ShapeDtypeStruct((2, self.group, c), jnp.bfloat16) for c in self.count
        ]
        self.scratch = [
            pltpu.VMEM((2, sum(self.count), self.wide), jnp.bfloat16),
            pltpu.VMEM((2, 4 * self.group, self.quarter), jnp.bfloat16),
            pltpu.SemaphoreType.DMA((len(self.moves),)),
        ]

    def copies(self, sources, rows, query, sems):
        out = []
        for i, (_, start, count, side, to, *_) in enumerate(self.moves):
            into = rows.at[side, pl.ds(to, count)] if side < 2 else query.at[side - 2, pl.ds(to, count)]
            out.append(pltpu.make_async_copy(sources[i].at[pl.ds(start, count)], into, sems.at[i]))
        return out

    def compute(self, place_ref, outs, rows, query, copies):
        group, quarter = self.group, self.quarter
        per = self.wide // quarter
        for copy, move in zip(copies, self.moves):
            if move[3] >= 2:
                copy.wait()
        for i, out in enumerate(outs):
            first = sum(self.count[:i])
            for copy, move in zip(copies, self.moves):
                if move[3] < 2 and first <= move[4] < first + self.count[i]:
                    copy.wait()
            for j in range(2):
                total = None
                for k in range(4):
                    spot = place_ref[1 + k]
                    columns = pl.ds(pl.multiple_of((spot % per) * quarter, quarter), quarter)
                    term = lax.dot_general(
                        query[j, k * group : (k + 1) * group, :],
                        rows[spot // per, first : first + self.count[i], columns],
                        (((1,), (1,)), ((), ())),
                        preferred_element_type=jnp.float32,
                    )
                    total = term if total is None else total + term
                out[j] = total.astype(out.dtype)


def score_call(place, parts, slots):
    scores = Scores(parts, slots)
    n, m = len(slots), len(scores.moves)

    def kernel(place_ref, *refs):
        outs = refs[m : m + n]
        rows, query, sems = refs[m + n :]

        @pl.when(place_ref[0] == 1)
        def _():
            copies = scores.copies(refs[:m], rows, query, sems)
            for copy, move in zip(copies, scores.moves):
                if move[3] >= 2:
                    copy.start()
            for copy, move in zip(copies, scores.moves):
                if move[3] < 2:
                    copy.start()
            scores.compute(place_ref, outs, rows, query, copies)

    smem = pl.BlockSpec(memory_space=pltpu.SMEM)
    hbm = pl.BlockSpec(memory_space=pltpu.HBM)
    vmem = pl.BlockSpec(memory_space=pltpu.VMEM)
    return pl.pallas_call(
        kernel,
        out_shape=scores.out_shape,
        in_specs=[smem] + [hbm] * m,
        out_specs=[vmem] * n,
        scratch_shapes=scores.scratch,
        compiler_params=pltpu.CompilerParams(vmem_limit_bytes=18 * 2**20),
        cost_estimate=pl.CostEstimate(flops=0, bytes_accessed=0, transcendentals=0),
    )(place, *scores.arrays)


def weigh_call(place, on_middle, on_ends, swapped, weights):
    group, count = swapped[0].shape

    def kernel(place_ref, *refs):
        late, core = place_ref[5], place_ref[6]
        weight, out = refs[6], refs[7]

        def put(i, block, own_rows):
            row = late if i == 0 else 1 - late
            column = core if own_rows else 1 - core
            across = pl.ds(pl.multiple_of(column * count, count), count)
            down = pl.ds(pl.multiple_of(row * group, group), group)
            out[down, across] = block.astype(jnp.float32) * weight[:, across]

        for i in range(2):
            pl.when(place_ref[0] == 1)(lambda i=i: put(i, refs[i][0], True))
            pl.when(place_ref[0] == 0)(lambda i=i: put(i, refs[2 + i][0], True))
            put(i, refs[4 + i][...], False)

    smem = pl.BlockSpec(memory_space=pltpu.SMEM)
    vmem = pl.BlockSpec(memory_space=pltpu.VMEM)
    return pl.pallas_call(
        kernel,
        out_shape=jax.ShapeDtypeStruct((2 * group, 2 * count), jnp.float32),
        in_specs=[smem] + [vmem] * 7,
        out_specs=vmem,
        cost_estimate=pl.CostEstimate(flops=0, bytes_accessed=0, transcendentals=0),
    )(place, *on_middle, *on_ends, *swapped, weights)


def after(values, *done):
    return lax.optimization_barrier(tuple(values) + done)[: len(values)]


def local_line(slab_grads, query_grads, example_weights, tile_owner):
    count, quarter = slab_grads.shape
    half, piece = count // 2, count // 4
    e = lax.axis_index("ex")
    f = lax.axis_index("feat")
    core = f % 2
    middle = jnp.logical_or(e == 1, e == 2)
    late = (e >= 2).astype(jnp.int32)

    def move(value, pairs):
        return lax.ppermute(value, "ex", pairs)

    def across(value):
        return lax.ppermute(value, "feat", ACROSS)

    def swap(value):
        return lax.ppermute(value, "feat", CORE)

    def across_on(value, which):
        pairs = [(p * 4 + g, p * 4 + (g ^ 2)) for p in which for g in range(4)]
        return lax.ppermute(value, ("ex", "feat"), pairs)

    def swap_on(value, which):
        pairs = [(p * 4 + g, p * 4 + (g ^ 1)) for p in which for g in range(4)]
        return lax.ppermute(value, ("ex", "feat"), pairs)

    mids, ends = (1, 2), (0, 3)

    def whole(a, b):
        return ([(a, 0, half)], [(b, 0, half)])

    slots = tile_owner.shape[1] // 4
    own_tiles = lax.dynamic_slice(tile_owner[0], (e * slots, 0), (slots, 2))
    tiles = jnp.concatenate([swap(own_tiles), own_tiles], axis=0)
    blocks = quarter // B
    valid = (tiles[:, :1] >= 0).astype(jnp.int32)
    tiles = jnp.maximum(tiles, 0)
    table = ((tiles // blocks) ^ f) * blocks + tiles % blocks
    table = jnp.concatenate([table, valid], axis=1)
    order = jnp.where(e == 2, jnp.array([2, 3, 1, 0]), jnp.array([1, 0, 2, 3])).astype(jnp.int32)
    place = jnp.concatenate(
        [
            middle.astype(jnp.int32)[None],
            order ^ f,
            late[None],
            core[None],
            jnp.array([4 * count], jnp.int32),
        ]
    )

    keep = lax.dynamic_slice(slab_grads, (core * half, 0), (half, quarter))
    give = lax.dynamic_slice(slab_grads, ((1 - core) * half, 0), (half, quarter))
    own = jnp.concatenate([keep, swap(give)], axis=1)
    q_half = query_grads.shape[0] // 2

    own_x = across(own)
    near = move(own, PAIR)
    inner = move(own, INNER)

    def halves(value, which):
        return lax.dynamic_slice(value, (which * q_half, 0), (q_half, quarter))

    q_mine, q_other = halves(query_grads, late), halves(query_grads, 1 - late)
    near, inner, own, own_x, q_mine, q_other, table = after(
        (near, inner, own, own_x, q_mine, q_other, table)
    )
    near_x = across(near)
    outer = move(near, INNER)
    inner_end = move(inner, TO_END)
    q_end_other = move(q_other, TO_MID)
    q_mine_sibling = swap(q_mine)
    sibling0, sum0 = tile_call(place, table, whole(own, own_x))

    inner, inner_end, outer, near, near_x, q_end_other, q_mine, sibling0, sum0 = after(
        (inner, inner_end, outer, near, near_x, q_end_other, q_mine, sibling0, sum0)
    )
    second = jnp.where(middle, outer, inner_end)
    second_x = across(second)
    outer_end = move(outer, TO_END)
    q_inner = move(q_other, INNER)
    q_far = move(q_end_other, INNER)
    q_end = move(q_mine, TO_MID)
    sibling1, sum1 = tile_call(place, table, whole(near, near_x), [sum0], sibling0)

    second, second_x, outer_end, inner, sum1, sibling1 = after(
        (second, second_x, outer_end, inner, sum1, sibling1)
    )
    third = jnp.where(middle, inner, outer_end)
    third_x = across(third)
    parts = [(q_mine, q_mine_sibling)] + [(x, swap(x)) for x in (q_end, q_inner, q_far)]
    slots3 = [whole(own, own_x), whole(near, near_x), whole(second, second_x)]
    r_own, r_near, r_outer = score_call(place, parts, slots3)
    far = move(r_outer, INNER)
    to_end = move(r_near, TO_END)
    sibling2, sum2 = tile_call(place, table, whole(second, second_x), [sum1], sibling1)
    third_sibling = swap(third)

    first = jnp.where(middle, r_own[1], to_end[1])
    third_x, to_end, far, sibling2, first = after((third_x, to_end, far, sibling2, first), sum2, r_own)
    first_sibling = swap(first)
    third_x_sibling = swap(third_x)
    (r_inner,) = score_call(place, parts, [whole(third, third_x)])
    sibling2 = swap(sibling2)
    r_inner, far = after((r_inner, far))
    to_far = move(far, TO_END)
    to_mid = move(r_inner, INNER)
    sibling2, third_x_sibling = after((sibling2, third_x_sibling), r_inner)
    (gram,) = tile_call(
        place,
        table,
        (
            [(third, 0, half), (third_sibling, 0, half, True)],
            [(third_x, 0, half), (third_x_sibling, 0, half, True)],
        ),
        [sum2, sibling2],
        part="own",
    )
    to_end, to_far, to_mid, gram = after((to_end, to_far, to_mid, gram))
    rest_sibling = swap(jnp.where(middle, to_mid[1], to_far[1]))
    scores = weigh_call(
        place,
        (r_own, to_mid),
        (to_end, to_far),
        (first_sibling, rest_sibling),
        example_weights[None, :],
    )
    return gram[None], scores


def solution(mesh):
    placed = (
        P(("grp", "ex"), "feat"),
        P(("grp", "feat"), "ex"),
        P(("grp", "ex")),
        P(("grp", "feat"), None, None),
    )

    line = mesh.shape["ex"] == 4 and mesh.shape["feat"] == 4
    return jax.shard_map(
        local_line if line else local_any,
        mesh=mesh,
        in_specs=placed,
        out_specs=(P(("grp", "feat"), "ex", None, None), P(("grp", "feat"), "ex")),
        check_vma=False,
    )
```

```python
import math

import jax
import jax.numpy as jnp
from jax import lax
from jax.experimental import pallas as pl
from jax.experimental.pallas import tpu as pltpu
from jax.sharding import PartitionSpec as P

B = 128


def select_blocks(blocks3, indices):
    block_ids = lax.broadcasted_iota(jnp.int32, (indices.shape[0], blocks3.shape[1]), 1)
    onehot = (indices[:, None] == block_ids).astype(jnp.bfloat16)
    chosen = jnp.einsum("tnb,gn->tgb", blocks3, onehot, preferred_element_type=jnp.float32)
    return chosen.astype(jnp.bfloat16)


def tile_terms(blocks3, subset):
    group_size = math.gcd(subset.shape[0], 8)
    groups = subset.reshape(-1, group_size, 2)

    def group_tiles(group):
        left_block = select_blocks(blocks3, group[:, 0])
        right_block = select_blocks(blocks3, group[:, 1])
        product = jnp.einsum(
            "tsi,tsj->sij", left_block, right_block, preferred_element_type=jnp.float32
        )
        return jnp.where((group[:, 0] >= 0)[:, None, None], product, jnp.float32(0.0))

    return lax.map(group_tiles, groups).reshape(-1, blocks3.shape[2], blocks3.shape[2])


def local_any(slab_grads, query_grads, example_weights, tile_owner):
    tile_table = tile_owner[0]
    tok_count = slab_grads.shape[0]
    slab_full = lax.all_gather(slab_grads, "feat", axis=1, tiled=True)
    blocks3 = slab_full.reshape(tok_count, slab_full.shape[1] // B, B)
    row_total = tok_count * lax.axis_size("ex")
    summed = lax.psum_scatter(
        tile_terms(blocks3, tile_table).astype(jnp.bfloat16), "ex", scatter_dimension=0, tiled=True
    ).astype(jnp.float32)
    gram = (summed / row_total)[None]
    summed = lax.dot_general(
        lax.all_gather(query_grads, "ex", axis=1, tiled=True),
        slab_full,
        (((1,), (1,)), ((), ())),
        preferred_element_type=jnp.float32,
    )
    scores = summed * example_weights[None, :]
    return (gram, scores)


PAIR = ((0, 1), (1, 0), (2, 3), (3, 2))
INNER = ((1, 2), (2, 1))
TO_END = ((1, 0), (2, 3))
TO_MID = ((0, 1), (3, 2))
END_TO_FAR_MID = ((0, 2), (3, 1))
MID_TO_FAR_END = ((1, 3), (2, 0))
CORE = ((0, 1), (1, 0), (2, 3), (3, 2))
ACROSS = ((0, 2), (2, 0), (1, 3), (3, 1))


def plan(batches, own_count):
    out = []
    for sides in batches:
        for side in range(2):
            at = own_count
            for given, start, count, *flip in sides[side]:
                for plane, array in zip((1, 0), given) if isinstance(given, tuple) else [(2, given)]:
                    wide = array.shape[1]
                    if any(flip):
                        out.append((array, start, count, side, at, 0, wide // 2, wide // 2, plane))
                        out.append((array, start, count, side, at, wide // 2, 0, wide // 2, plane))
                    else:
                        out.append((array, start, count, side, at, 0, 0, wide, plane))
                at += count
    return out


def rows_of(batches):
    return sum(entry[2] for sides in batches[:1] for entry in sides[0])


def tile_call(place, table, always, carried=(), carried_sibling=None, part="both", scores=None):
    tiles = table.shape[0]
    moves = [plan([always], 0)]
    arrays = []
    for some in moves:
        for array, *_ in some:
            if not any(array is x for x in arrays):
                arrays.append(array)
    where = [[next(i for i, x in enumerate(arrays) if x is m[0]) for m in some] for some in moves]
    n = len(arrays)
    n_moves = sum(len(some) for some in moves)
    wide = arrays[0].shape[1]
    total = rows_of([always])
    half = tiles // 2
    per = wide // B
    extra = [] if carried_sibling is None else [carried_sibling]
    carried = list(carried) + extra
    n_own = len(carried) - len(extra)
    unroll = max(u for u in range(1, 22) if half // 2 % u == 0)
    n_out = 2 if part == "both" else 1

    n_scores = len(scores.count) if scores else 0
    score_arrays = scores.arrays if scores else []
    n_in = n + len(carried) + len(score_arrays)

    def kernel(place_ref, table_ref, *refs):
        score_sources = refs[n + len(carried) : n_in]
        score_outs = refs[n_in + n_out : n_in + n_out + n_scores]
        refs = refs[: n + len(carried)] + refs[n_in : n_in + n_out] + refs[n_in + n_out + n_scores :]
        if scores:
            score_scratch, refs = refs[-3:], refs[:-3]
            score_copies = scores.copies(score_sources, *score_scratch)
        row_refs = refs[:n]
        carried_refs = refs[n : n + len(carried)]
        out_refs = refs[n + len(carried) : n + len(carried) + n_out]
        outs = refs[n + len(carried) + n_out : -3 - len(carried)]
        held = refs[-3 - len(carried) : -3]
        rows, turned, sems = refs[-3:]
        held_copies = [
            pltpu.make_async_copy(ref, held[i], sems.at[n_moves + i])
            for i, ref in enumerate(carried_refs)
        ]
        parts = []
        for i in range(n_out):
            for j in range(2):
                some = pl.ds(j * (half // 2), half // 2)
                sem = sems.at[n_moves + len(carried) + 2 * i + j]
                parts.append(pltpu.make_async_copy(outs[i].at[some], out_refs[i].at[some], sem))
        copies = [[], [], []]
        at = 0
        for i, some in enumerate(moves):
            for (_, start, count, side, to, left, right, columns, plane), index in zip(some, where[i]):
                source = row_refs[index].at[pl.ds(start, count), pl.ds(left, columns)]
                into = rows.at[side, pl.ds(to, count), pl.ds(right, columns)]
                copies[plane].append(pltpu.make_async_copy(source, into, sems.at[at]))
                at += 1

        def each(some, do):
            for copy in some:
                do(copy)

        def rows_do(do):
            each(copies[2], do)
            for plane in range(2):
                if copies[plane]:
                    pl.when(place_ref[0] == plane)(lambda plane=plane: each(copies[plane], do))

        rows_do(lambda copy: copy.start())
        each(held_copies, lambda copy: copy.start())
        if scores:
            pl.when(place_ref[0] == 1)(lambda: each(score_copies, lambda copy: copy.start()))
        rows_do(lambda copy: copy.wait())

        for block in range(2 * per):
            side, column = divmod(block * B, wide)
            turned[block] = rows[side, :, column : column + B].T

        def product(tile):
            right = table_ref[tile, 1]
            return jnp.dot(
                turned[table_ref[tile, 0]],
                rows[right // per, :, pl.ds(pl.multiple_of((right % per) * B, B), B)],
                preferred_element_type=jnp.float32,
            )

        def sibling(tile, _):
            sum_ = product(tile)
            for ref in held[n_own:]:
                sum_ += ref[tile].astype(jnp.float32)
            outs[0][tile] = sum_.astype(outs[0].dtype)
            return 0

        def mine(tile, _):
            sum_ = product(tile + half)
            for ref in held[:n_own]:
                sum_ += ref[tile].astype(jnp.float32)
            if part == "own":
                scale = 1.0 / place_ref[7].astype(jnp.float32)
                sum_ = sum_ * jnp.where(table_ref[tile + half, 2] == 1, scale, 0.0)
            outs[-1][tile] = sum_
            return 0

        if part != "own":
            for copy in held_copies[n_own:]:
                copy.wait()
            for j in range(2):
                lax.fori_loop(j * (half // 2), (j + 1) * (half // 2), sibling, 0, unroll=unroll)
                parts[j].start()
        if part != "sibling":
            for copy in held_copies[:n_own]:
                copy.wait()
            for j in range(2):
                lax.fori_loop(j * (half // 2), (j + 1) * (half // 2), mine, 0, unroll=unroll)
                parts[j - 2].start()
        if scores:

            @pl.when(place_ref[0] == 1)
            def _():
                scores.compute(place_ref, score_outs, *score_scratch[:2], score_copies)

        for copy in parts:
            copy.wait()

    smem = pl.BlockSpec(memory_space=pltpu.SMEM)
    hbm = pl.BlockSpec(memory_space=pltpu.HBM)
    outs = []
    if part != "own":
        outs.append(jax.ShapeDtypeStruct((half, B, B), jnp.bfloat16))
    if part != "sibling":
        outs.append(jax.ShapeDtypeStruct((half, B, B), jnp.float32))
    return pl.pallas_call(
        kernel,
        out_shape=outs + (scores.out_shape if scores else []),
        in_specs=[smem, smem] + [hbm] * n_in,
        out_specs=[hbm] * n_out + [pl.BlockSpec(memory_space=pltpu.VMEM)] * n_scores,
        scratch_shapes=[pltpu.VMEM(x.shape, x.dtype) for x in outs + list(carried)]
        + [
            pltpu.VMEM((2, total, wide), jnp.bfloat16),
            pltpu.VMEM((2 * per, B, total), jnp.bfloat16),
            pltpu.SemaphoreType.DMA((n_moves + len(carried) + 2 * n_out,)),
        ]
        + (scores.scratch if scores else []),
        compiler_params=pltpu.CompilerParams(vmem_limit_bytes=18 * 2**20),
        cost_estimate=pl.CostEstimate(flops=0, bytes_accessed=0, transcendentals=0),
    )(place, table, *arrays, *carried, *score_arrays)


class Scores:
    def __init__(self, parts, slots):
        self.count = [rows_of([slot]) for slot in slots]
        self.moves = []
        for i, slot in enumerate(slots):
            self.moves += plan([slot], sum(self.count[:i]))
        self.quarter = parts[0][0].shape[1]
        lengths = [pair[0].shape[0] for pair in parts]
        for i, pair in enumerate(parts):
            for j in range(2):
                at = sum(lengths[:i])
                self.moves.append((pair[j], 0, lengths[i], 2 + j, at, 0, 0, self.quarter, 2))
        self.wide = self.moves[0][0].shape[1]
        self.group = sum(lengths) // 4
        self.arrays = [move[0] for move in self.moves]
        self.out_shape = [
            jax.ShapeDtypeStruct((2, self.group, c), jnp.bfloat16) for c in self.count
        ]
        self.scratch = [
            pltpu.VMEM((2, sum(self.count), self.wide), jnp.bfloat16),
            pltpu.VMEM((2, 4 * self.group, self.quarter), jnp.bfloat16),
            pltpu.SemaphoreType.DMA((len(self.moves),)),
        ]

    def copies(self, sources, rows, query, sems):
        out = []
        for i, (_, start, count, side, to, *_) in enumerate(self.moves):
            into = rows.at[side, pl.ds(to, count)] if side < 2 else query.at[side - 2, pl.ds(to, count)]
            out.append(pltpu.make_async_copy(sources[i].at[pl.ds(start, count)], into, sems.at[i]))
        return out

    def compute(self, place_ref, outs, rows, query, copies):
        group, quarter = self.group, self.quarter
        per = self.wide // quarter
        for copy, move in zip(copies, self.moves):
            if move[3] >= 2:
                copy.wait()
        for i, out in enumerate(outs):
            first = sum(self.count[:i])
            for copy, move in zip(copies, self.moves):
                if move[3] < 2 and first <= move[4] < first + self.count[i]:
                    copy.wait()
            for j in range(2):
                total = None
                for k in range(4):
                    spot = place_ref[1 + k]
                    columns = pl.ds(pl.multiple_of((spot % per) * quarter, quarter), quarter)
                    term = lax.dot_general(
                        query[j, k * group : (k + 1) * group, :],
                        rows[spot // per, first : first + self.count[i], columns],
                        (((1,), (1,)), ((), ())),
                        preferred_element_type=jnp.float32,
                    )
                    total = term if total is None else total + term
                out[j] = total.astype(out.dtype)


def score_call(place, parts, slots):
    scores = Scores(parts, slots)
    n, m = len(slots), len(scores.moves)

    def kernel(place_ref, *refs):
        outs = refs[m : m + n]
        rows, query, sems = refs[m + n :]

        @pl.when(place_ref[0] == 1)
        def _():
            copies = scores.copies(refs[:m], rows, query, sems)
            for copy, move in zip(copies, scores.moves):
                if move[3] >= 2:
                    copy.start()
            for copy, move in zip(copies, scores.moves):
                if move[3] < 2:
                    copy.start()
            scores.compute(place_ref, outs, rows, query, copies)

    smem = pl.BlockSpec(memory_space=pltpu.SMEM)
    hbm = pl.BlockSpec(memory_space=pltpu.HBM)
    vmem = pl.BlockSpec(memory_space=pltpu.VMEM)
    return pl.pallas_call(
        kernel,
        out_shape=scores.out_shape,
        in_specs=[smem] + [hbm] * m,
        out_specs=[vmem] * n,
        scratch_shapes=scores.scratch,
        compiler_params=pltpu.CompilerParams(vmem_limit_bytes=18 * 2**20),
        cost_estimate=pl.CostEstimate(flops=0, bytes_accessed=0, transcendentals=0),
    )(place, *scores.arrays)


def weigh_call(place, on_middle, on_ends, swapped, weights):
    group, count = swapped[0].shape

    def kernel(place_ref, *refs):
        late, core = place_ref[5], place_ref[6]
        weight, out = refs[6], refs[7]

        def put(i, block, own_rows):
            row = late if i == 0 else 1 - late
            column = core if own_rows else 1 - core
            across = pl.ds(pl.multiple_of(column * count, count), count)
            down = pl.ds(pl.multiple_of(row * group, group), group)
            out[down, across] = block.astype(jnp.float32) * weight[:, across]

        for i in range(2):
            pl.when(place_ref[0] == 1)(lambda i=i: put(i, refs[i][0], True))
            pl.when(place_ref[0] == 0)(lambda i=i: put(i, refs[2 + i][0], True))
            put(i, refs[4 + i][...], False)

    smem = pl.BlockSpec(memory_space=pltpu.SMEM)
    vmem = pl.BlockSpec(memory_space=pltpu.VMEM)
    return pl.pallas_call(
        kernel,
        out_shape=jax.ShapeDtypeStruct((2 * group, 2 * count), jnp.float32),
        in_specs=[smem] + [vmem] * 7,
        out_specs=vmem,
        compiler_params=pltpu.CompilerParams(vmem_limit_bytes=8 * 2**20),
        cost_estimate=pl.CostEstimate(flops=0, bytes_accessed=0, transcendentals=0),
    )(place, *on_middle, *on_ends, *swapped, weights)


def after(values, *done):
    return lax.optimization_barrier(tuple(values) + done)[: len(values)]


def local_line(slab_grads, query_grads, example_weights, tile_owner):
    count, quarter = slab_grads.shape
    half, piece = count // 2, count // 4
    e = lax.axis_index("ex")
    f = lax.axis_index("feat")
    core = f % 2
    middle = jnp.logical_or(e == 1, e == 2)
    late = (e >= 2).astype(jnp.int32)

    def move(value, pairs):
        return lax.ppermute(value, "ex", pairs)

    def across(value):
        return lax.ppermute(value, "feat", ACROSS)

    def swap(value):
        return lax.ppermute(value, "feat", CORE)

    def across_on(value, which):
        pairs = [(p * 4 + g, p * 4 + (g ^ 2)) for p in which for g in range(4)]
        return lax.ppermute(value, ("ex", "feat"), pairs)

    def swap_on(value, which):
        pairs = [(p * 4 + g, p * 4 + (g ^ 1)) for p in which for g in range(4)]
        return lax.ppermute(value, ("ex", "feat"), pairs)

    mids, ends = (1, 2), (0, 3)

    def whole(a, b):
        return ([(a, 0, half)], [(b, 0, half)])

    slots = tile_owner.shape[1] // 4
    own_tiles = lax.dynamic_slice(tile_owner[0], (e * slots, 0), (slots, 2))
    tiles = jnp.concatenate([swap(own_tiles), own_tiles], axis=0)
    blocks = quarter // B
    valid = (tiles[:, :1] >= 0).astype(jnp.int32)
    tiles = jnp.maximum(tiles, 0)
    table = ((tiles // blocks) ^ f) * blocks + tiles % blocks
    table = jnp.concatenate([table, valid], axis=1)
    order = jnp.where(e == 2, jnp.array([2, 3, 1, 0]), jnp.array([1, 0, 2, 3])).astype(jnp.int32)
    place = jnp.concatenate(
        [
            middle.astype(jnp.int32)[None],
            order ^ f,
            late[None],
            core[None],
            jnp.array([4 * count], jnp.int32),
        ]
    )

    keep = lax.dynamic_slice(slab_grads, (core * half, 0), (half, quarter))
    give = lax.dynamic_slice(slab_grads, ((1 - core) * half, 0), (half, quarter))
    own = jnp.concatenate([keep, swap(give)], axis=1)
    q_half = query_grads.shape[0] // 2

    own_x = across(own)
    near = move(own, PAIR)
    inner = move(own, INNER)

    def halves(value, which):
        return lax.dynamic_slice(value, (which * q_half, 0), (q_half, quarter))

    q_mine, q_other = halves(query_grads, late), halves(query_grads, 1 - late)
    near, inner, own, own_x, q_mine, q_other, table = after(
        (near, inner, own, own_x, q_mine, q_other, table)
    )
    near_x = across(near)
    outer = move(near, INNER)
    inner_end = move(inner, TO_END)
    q_end_other = move(q_other, TO_MID)
    q_mine_sibling = swap(q_mine)
    sibling0, sum0 = tile_call(place, table, whole(own, own_x))

    inner, inner_end, outer, near, near_x, q_end_other, q_mine, sibling0, sum0 = after(
        (inner, inner_end, outer, near, near_x, q_end_other, q_mine, sibling0, sum0)
    )
    second = jnp.where(middle, outer, inner_end)
    second_x = across(second)
    outer_end = move(outer, TO_END)
    q_inner = move(q_other, INNER)
    q_far = move(q_end_other, INNER)
    q_end = move(q_mine, TO_MID)
    sibling1, sum1 = tile_call(place, table, whole(near, near_x), [sum0], sibling0)

    second, second_x, outer_end, inner, sum1, sibling1 = after(
        (second, second_x, outer_end, inner, sum1, sibling1)
    )
    third = jnp.where(middle, inner, outer_end)
    third_x = across(third)
    parts = [(q_mine, q_mine_sibling)] + [(x, swap(x)) for x in (q_end, q_inner, q_far)]
    slots3 = [whole(own, own_x), whole(near, near_x), whole(second, second_x)]
    r_own, r_near, r_outer = score_call(place, parts, slots3)
    far = move(r_outer, INNER)
    to_end = move(r_near, TO_END)
    sibling2, sum2 = tile_call(place, table, whole(second, second_x), [sum1], sibling1)
    third_sibling = swap(third)

    first = jnp.where(middle, r_own[1], to_end[1])
    third_x, to_end, far, sibling2, first = after((third_x, to_end, far, sibling2, first), sum2, r_own)
    first_sibling = swap(first)
    third_x_sibling = swap(third_x)
    (r_inner,) = score_call(place, parts, [whole(third, third_x)])
    sibling2 = swap(sibling2)
    r_inner, far = after((r_inner, far))
    to_far = move(far, TO_END)
    to_mid = move(r_inner, INNER)
    sibling2, third_x_sibling = after((sibling2, third_x_sibling), r_inner)
    (gram,) = tile_call(
        place,
        table,
        (
            [(third, 0, half), (third_sibling, 0, half, True)],
            [(third_x, 0, half), (third_x_sibling, 0, half, True)],
        ),
        [sum2, sibling2],
        part="own",
    )
    to_end, to_far, to_mid, gram = after((to_end, to_far, to_mid, gram))
    rest_sibling = swap(jnp.where(middle, to_mid[1], to_far[1]))
    scores = weigh_call(
        place,
        (r_own, to_mid),
        (to_end, to_far),
        (first_sibling, rest_sibling),
        example_weights[None, :],
    )
    return gram[None], scores


def solution(mesh):
    placed = (
        P(("grp", "ex"), "feat"),
        P(("grp", "feat"), "ex"),
        P(("grp", "ex")),
        P(("grp", "feat"), None, None),
    )

    line = mesh.shape["ex"] == 4 and mesh.shape["feat"] == 4
    return jax.shard_map(
        local_line if line else local_any,
        mesh=mesh,
        in_specs=placed,
        out_specs=(P(("grp", "feat"), "ex", None, None), P(("grp", "feat"), "ex")),
        check_vma=False,
    )
```

```python
import math

import jax
import jax.numpy as jnp
from jax import lax
from jax.experimental import pallas as pl
from jax.experimental.pallas import tpu as pltpu
from jax.sharding import PartitionSpec as P

B = 128


def select_blocks(blocks3, indices):
    block_ids = lax.broadcasted_iota(jnp.int32, (indices.shape[0], blocks3.shape[1]), 1)
    onehot = (indices[:, None] == block_ids).astype(jnp.bfloat16)
    chosen = jnp.einsum("tnb,gn->tgb", blocks3, onehot, preferred_element_type=jnp.float32)
    return chosen.astype(jnp.bfloat16)


def tile_terms(blocks3, subset):
    group_size = math.gcd(subset.shape[0], 8)
    groups = subset.reshape(-1, group_size, 2)

    def group_tiles(group):
        left_block = select_blocks(blocks3, group[:, 0])
        right_block = select_blocks(blocks3, group[:, 1])
        product = jnp.einsum(
            "tsi,tsj->sij", left_block, right_block, preferred_element_type=jnp.float32
        )
        return jnp.where((group[:, 0] >= 0)[:, None, None], product, jnp.float32(0.0))

    return lax.map(group_tiles, groups).reshape(-1, blocks3.shape[2], blocks3.shape[2])


def local_any(slab_grads, query_grads, example_weights, tile_owner):
    tile_table = tile_owner[0]
    tok_count = slab_grads.shape[0]
    slab_full = lax.all_gather(slab_grads, "feat", axis=1, tiled=True)
    blocks3 = slab_full.reshape(tok_count, slab_full.shape[1] // B, B)
    row_total = tok_count * lax.axis_size("ex")
    summed = lax.psum_scatter(
        tile_terms(blocks3, tile_table).astype(jnp.bfloat16), "ex", scatter_dimension=0, tiled=True
    ).astype(jnp.float32)
    gram = (summed / row_total)[None]
    summed = lax.dot_general(
        lax.all_gather(query_grads, "ex", axis=1, tiled=True),
        slab_full,
        (((1,), (1,)), ((), ())),
        preferred_element_type=jnp.float32,
    )
    scores = summed * example_weights[None, :]
    return (gram, scores)


PAIR = ((0, 1), (1, 0), (2, 3), (3, 2))
INNER = ((1, 2), (2, 1))
TO_END = ((1, 0), (2, 3))
TO_MID = ((0, 1), (3, 2))
END_TO_FAR_MID = ((0, 2), (3, 1))
MID_TO_FAR_END = ((1, 3), (2, 0))
CORE = ((0, 1), (1, 0), (2, 3), (3, 2))
ACROSS = ((0, 2), (2, 0), (1, 3), (3, 1))


def plan(batches, own_count):
    out = []
    for sides in batches:
        for side in range(2):
            at = own_count
            for given, start, count, *flip in sides[side]:
                for plane, array in zip((1, 0), given) if isinstance(given, tuple) else [(2, given)]:
                    wide = array.shape[1]
                    if any(flip):
                        out.append((array, start, count, side, at, 0, wide // 2, wide // 2, plane))
                        out.append((array, start, count, side, at, wide // 2, 0, wide // 2, plane))
                    else:
                        out.append((array, start, count, side, at, 0, 0, wide, plane))
                at += count
    return out


def rows_of(batches):
    return sum(entry[2] for sides in batches[:1] for entry in sides[0])


def tile_call(place, table, always, carried=(), carried_sibling=None, part="both", scores=None):
    tiles = table.shape[0]
    moves = [plan([always], 0)]
    arrays = []
    for some in moves:
        for array, *_ in some:
            if not any(array is x for x in arrays):
                arrays.append(array)
    where = [[next(i for i, x in enumerate(arrays) if x is m[0]) for m in some] for some in moves]
    n = len(arrays)
    n_moves = sum(len(some) for some in moves)
    wide = arrays[0].shape[1]
    total = rows_of([always])
    half = tiles // 2
    per = wide // B
    extra = [] if carried_sibling is None else [carried_sibling]
    carried = list(carried) + extra
    n_own = len(carried) - len(extra)
    unroll = max(u for u in range(1, 22) if half // 2 % u == 0)
    n_out = 2 if part == "both" else 1
    inside = part == "both"

    n_scores = len(scores.count) if scores else 0
    score_arrays = scores.arrays if scores else []
    n_in = n + len(carried) + len(score_arrays)

    def kernel(place_ref, table_ref, *refs):
        score_sources = refs[n + len(carried) : n_in]
        score_outs = refs[n_in + n_out : n_in + n_out + n_scores]
        refs = refs[: n + len(carried)] + refs[n_in : n_in + n_out] + refs[n_in + n_out + n_scores :]
        if scores:
            score_scratch, refs = refs[-3:], refs[:-3]
            score_copies = scores.copies(score_sources, *score_scratch)
        row_refs = refs[:n]
        carried_refs = refs[n : n + len(carried)]
        out_refs = refs[n + len(carried) : n + len(carried) + n_out]
        outs = out_refs if inside else refs[n + len(carried) + n_out : -3]
        held = carried_refs
        rows, turned, sems = refs[-3:]
        parts = []
        for i in range(0 if inside else n_out):
            for j in range(2):
                some = pl.ds(j * (half // 2), half // 2)
                sem = sems.at[n_moves + len(carried) + 2 * i + j]
                parts.append(pltpu.make_async_copy(outs[i].at[some], out_refs[i].at[some], sem))
        copies = [[], [], []]
        at = 0
        for i, some in enumerate(moves):
            for (_, start, count, side, to, left, right, columns, plane), index in zip(some, where[i]):
                source = row_refs[index].at[pl.ds(start, count), pl.ds(left, columns)]
                into = rows.at[side, pl.ds(to, count), pl.ds(right, columns)]
                copies[plane].append(pltpu.make_async_copy(source, into, sems.at[at]))
                at += 1

        def each(some, do):
            for copy in some:
                do(copy)

        def rows_do(do):
            each(copies[2], do)
            for plane in range(2):
                if copies[plane]:
                    pl.when(place_ref[0] == plane)(lambda plane=plane: each(copies[plane], do))

        rows_do(lambda copy: copy.start())
        if scores:
            pl.when(place_ref[0] == 1)(lambda: each(score_copies, lambda copy: copy.start()))
        rows_do(lambda copy: copy.wait())

        for block in range(2 * per):
            side, column = divmod(block * B, wide)
            turned[block] = rows[side, :, column : column + B].T

        def product(tile):
            right = table_ref[tile, 1]
            return jnp.dot(
                turned[table_ref[tile, 0]],
                rows[right // per, :, pl.ds(pl.multiple_of((right % per) * B, B), B)],
                preferred_element_type=jnp.float32,
            )

        def sibling(tile, _):
            sum_ = product(tile)
            for ref in held[n_own:]:
                sum_ += ref[tile].astype(jnp.float32)
            outs[0][tile] = sum_.astype(outs[0].dtype)
            return 0

        def mine(tile, _):
            sum_ = product(tile + half)
            for ref in held[:n_own]:
                sum_ += ref[tile].astype(jnp.float32)
            if part == "own":
                scale = 1.0 / place_ref[7].astype(jnp.float32)
                sum_ = sum_ * jnp.where(table_ref[tile + half, 2] == 1, scale, 0.0)
            outs[-1][tile] = sum_
            return 0

        if part != "own":
            for j in range(2):
                lax.fori_loop(j * (half // 2), (j + 1) * (half // 2), sibling, 0, unroll=unroll)
                if parts:
                    parts[j].start()
        if part != "sibling":
            for j in range(2):
                lax.fori_loop(j * (half // 2), (j + 1) * (half // 2), mine, 0, unroll=unroll)
                if parts:
                    parts[j - 2].start()
        if scores:

            @pl.when(place_ref[0] == 1)
            def _():
                scores.compute(place_ref, score_outs, *score_scratch[:2], score_copies)

        for copy in parts:
            copy.wait()

    smem = pl.BlockSpec(memory_space=pltpu.SMEM)
    hbm = pl.BlockSpec(memory_space=pltpu.HBM)
    vmem = pl.BlockSpec(memory_space=pltpu.VMEM)
    outs = []
    if part != "own":
        outs.append(jax.ShapeDtypeStruct((half, B, B), jnp.bfloat16))
    if part != "sibling":
        outs.append(jax.ShapeDtypeStruct((half, B, B), jnp.float32))
    return pl.pallas_call(
        kernel,
        out_shape=outs + (scores.out_shape if scores else []),
        in_specs=[smem, smem] + [hbm] * n + [vmem] * len(carried) + [hbm] * len(score_arrays),
        out_specs=[vmem if inside else hbm] * n_out + [pl.BlockSpec(memory_space=pltpu.VMEM)] * n_scores,
        scratch_shapes=[pltpu.VMEM(x.shape, x.dtype) for x in outs if not inside]
        + [
            pltpu.VMEM((2, total, wide), jnp.bfloat16),
            pltpu.VMEM((2 * per, B, total), jnp.bfloat16),
            pltpu.SemaphoreType.DMA((n_moves + len(carried) + 2 * n_out,)),
        ]
        + (scores.scratch if scores else []),
        compiler_params=pltpu.CompilerParams(vmem_limit_bytes=13 * 2**20),
        cost_estimate=pl.CostEstimate(flops=0, bytes_accessed=0, transcendentals=0),
    )(place, table, *arrays, *carried, *score_arrays)


class Scores:
    def __init__(self, parts, slots):
        self.count = [rows_of([slot]) for slot in slots]
        self.moves = []
        for i, slot in enumerate(slots):
            self.moves += plan([slot], sum(self.count[:i]))
        self.quarter = parts[0][0].shape[1]
        lengths = [pair[0].shape[0] for pair in parts]
        self.queries = [x for pair in parts for x in pair]
        self.wide = self.moves[0][0].shape[1]
        self.group = sum(lengths) // 4
        self.arrays = [move[0] for move in self.moves]
        self.out_shape = [
            jax.ShapeDtypeStruct((2, self.group, c), jnp.bfloat16) for c in self.count
        ]
        self.scratch = [
            pltpu.VMEM((2, sum(self.count), self.wide), jnp.bfloat16),
            pltpu.SemaphoreType.DMA((len(self.moves),)),
        ]

    def copies(self, sources, rows, sems):
        out = []
        for i, (_, start, count, side, to, *_) in enumerate(self.moves):
            into = rows.at[side, pl.ds(to, count)]
            out.append(pltpu.make_async_copy(sources[i].at[pl.ds(start, count)], into, sems.at[i]))
        return out

    def compute(self, place_ref, outs, rows, query, copies):
        group, quarter = self.group, self.quarter
        per = self.wide // quarter
        for i, out in enumerate(outs):
            first = sum(self.count[:i])
            for copy, move in zip(copies, self.moves):
                if move[3] < 2 and first <= move[4] < first + self.count[i]:
                    copy.wait()
            for j in range(2):
                total = None
                for k in range(4):
                    spot = place_ref[1 + k]
                    columns = pl.ds(pl.multiple_of((spot % per) * quarter, quarter), quarter)
                    term = lax.dot_general(
                        query[2 * k + j][...],
                        rows[spot // per, first : first + self.count[i], columns],
                        (((1,), (1,)), ((), ())),
                        preferred_element_type=jnp.float32,
                    )
                    total = term if total is None else total + term
                out[j] = total.astype(out.dtype)


def score_call(place, parts, slots):
    scores = Scores(parts, slots)
    n, m = len(slots), len(scores.moves)

    def kernel(place_ref, *refs):
        outs = refs[m + 8 : m + 8 + n]
        rows, sems = refs[m + 8 + n :]

        @pl.when(place_ref[0] == 1)
        def _():
            copies = scores.copies(refs[:m], rows, sems)
            for copy in copies:
                copy.start()
            scores.compute(place_ref, outs, rows, refs[m : m + 8], copies)

    smem = pl.BlockSpec(memory_space=pltpu.SMEM)
    hbm = pl.BlockSpec(memory_space=pltpu.HBM)
    vmem = pl.BlockSpec(memory_space=pltpu.VMEM)
    return pl.pallas_call(
        kernel,
        out_shape=scores.out_shape,
        in_specs=[smem] + [hbm] * m + [vmem] * 8,
        out_specs=[vmem] * n,
        scratch_shapes=scores.scratch,
        compiler_params=pltpu.CompilerParams(vmem_limit_bytes=9 * 2**20),
        cost_estimate=pl.CostEstimate(flops=0, bytes_accessed=0, transcendentals=0),
    )(place, *scores.arrays, *scores.queries)


def weigh_call(place, on_middle, on_ends, swapped, weights):
    group, count = swapped[0].shape

    def kernel(place_ref, *refs):
        late, core = place_ref[5], place_ref[6]
        weight, out = refs[6], refs[7]

        def put(i, block, own_rows):
            row = late if i == 0 else 1 - late
            column = core if own_rows else 1 - core
            across = pl.ds(pl.multiple_of(column * count, count), count)
            down = pl.ds(pl.multiple_of(row * group, group), group)
            out[down, across] = block.astype(jnp.float32) * weight[:, across]

        for i in range(2):
            pl.when(place_ref[0] == 1)(lambda i=i: put(i, refs[i][0], True))
            pl.when(place_ref[0] == 0)(lambda i=i: put(i, refs[2 + i][0], True))
            put(i, refs[4 + i][...], False)

    smem = pl.BlockSpec(memory_space=pltpu.SMEM)
    vmem = pl.BlockSpec(memory_space=pltpu.VMEM)
    return pl.pallas_call(
        kernel,
        out_shape=jax.ShapeDtypeStruct((2 * group, 2 * count), jnp.float32),
        in_specs=[smem] + [vmem] * 7,
        out_specs=vmem,
        compiler_params=pltpu.CompilerParams(vmem_limit_bytes=8 * 2**20),
        cost_estimate=pl.CostEstimate(flops=0, bytes_accessed=0, transcendentals=0),
    )(place, *on_middle, *on_ends, *swapped, weights)


def after(values, *done):
    return lax.optimization_barrier(tuple(values) + done)[: len(values)]


def local_line(slab_grads, query_grads, example_weights, tile_owner):
    count, quarter = slab_grads.shape
    half, piece = count // 2, count // 4
    e = lax.axis_index("ex")
    f = lax.axis_index("feat")
    core = f % 2
    middle = jnp.logical_or(e == 1, e == 2)
    late = (e >= 2).astype(jnp.int32)

    def move(value, pairs):
        return lax.ppermute(value, "ex", pairs)

    def across(value):
        return lax.ppermute(value, "feat", ACROSS)

    def swap(value):
        return lax.ppermute(value, "feat", CORE)

    def across_on(value, which):
        pairs = [(p * 4 + g, p * 4 + (g ^ 2)) for p in which for g in range(4)]
        return lax.ppermute(value, ("ex", "feat"), pairs)

    def swap_on(value, which):
        pairs = [(p * 4 + g, p * 4 + (g ^ 1)) for p in which for g in range(4)]
        return lax.ppermute(value, ("ex", "feat"), pairs)

    mids, ends = (1, 2), (0, 3)

    def whole(a, b):
        return ([(a, 0, half)], [(b, 0, half)])

    slots = tile_owner.shape[1] // 4
    own_tiles = lax.dynamic_slice(tile_owner[0], (e * slots, 0), (slots, 2))
    tiles = jnp.concatenate([swap(own_tiles), own_tiles], axis=0)
    blocks = quarter // B
    valid = (tiles[:, :1] >= 0).astype(jnp.int32)
    tiles = jnp.maximum(tiles, 0)
    table = ((tiles // blocks) ^ f) * blocks + tiles % blocks
    table = jnp.concatenate([table, valid], axis=1)
    order = jnp.where(e == 2, jnp.array([2, 3, 1, 0]), jnp.array([1, 0, 2, 3])).astype(jnp.int32)
    place = jnp.concatenate(
        [
            middle.astype(jnp.int32)[None],
            order ^ f,
            late[None],
            core[None],
            jnp.array([4 * count], jnp.int32),
        ]
    )

    keep = lax.dynamic_slice(slab_grads, (core * half, 0), (half, quarter))
    give = lax.dynamic_slice(slab_grads, ((1 - core) * half, 0), (half, quarter))
    own = jnp.concatenate([keep, swap(give)], axis=1)
    q_half = query_grads.shape[0] // 2

    own_x = across(own)
    near = move(own, PAIR)
    inner = move(own, INNER)

    def halves(value, which):
        return lax.dynamic_slice(value, (which * q_half, 0), (q_half, quarter))

    q_mine, q_other = halves(query_grads, late), halves(query_grads, 1 - late)
    near, inner, own, own_x, q_mine, q_other, table = after(
        (near, inner, own, own_x, q_mine, q_other, table)
    )
    near_x = across(near)
    outer = move(near, INNER)
    inner_end = move(inner, TO_END)
    q_end_other = move(q_other, TO_MID)
    q_mine_sibling = swap(q_mine)
    sibling0, sum0 = tile_call(place, table, whole(own, own_x))

    inner, inner_end, outer, near, near_x, q_end_other, q_mine, sibling0, sum0 = after(
        (inner, inner_end, outer, near, near_x, q_end_other, q_mine, sibling0, sum0)
    )
    second = jnp.where(middle, outer, inner_end)
    second_x = across(second)
    outer_end = move(outer, TO_END)
    q_inner = move(q_other, INNER)
    q_far = move(q_end_other, INNER)
    q_end = move(q_mine, TO_MID)
    sibling1, sum1 = tile_call(place, table, whole(near, near_x), [sum0], sibling0)

    second, second_x, outer_end, inner, sum1, sibling1 = after(
        (second, second_x, outer_end, inner, sum1, sibling1)
    )
    third = jnp.where(middle, inner, outer_end)
    third_x = across(third)
    parts = [(q_mine, q_mine_sibling)] + [(x, swap(x)) for x in (q_end, q_inner, q_far)]
    slots3 = [whole(own, own_x), whole(near, near_x), whole(second, second_x)]
    r_own, r_near, r_outer = score_call(place, parts, slots3)
    far = move(r_outer, INNER)
    to_end = move(r_near, TO_END)
    sibling2, sum2 = tile_call(place, table, whole(second, second_x), [sum1], sibling1)
    third_sibling = swap(third)

    first = jnp.where(middle, r_own[1], to_end[1])
    third_x, to_end, far, sibling2, first = after((third_x, to_end, far, sibling2, first), sum2, r_own)
    first_sibling = swap(first)
    third_x_sibling = swap(third_x)
    (r_inner,) = score_call(place, parts, [whole(third, third_x)])
    sibling2 = swap(sibling2)
    r_inner, far = after((r_inner, far))
    to_far = move(far, TO_END)
    to_mid = move(r_inner, INNER)
    sibling2, third_x_sibling = after((sibling2, third_x_sibling), r_inner)
    (gram,) = tile_call(
        place,
        table,
        (
            [(third, 0, half), (third_sibling, 0, half, True)],
            [(third_x, 0, half), (third_x_sibling, 0, half, True)],
        ),
        [sum2, sibling2],
        part="own",
    )
    to_end, to_far, to_mid, gram = after((to_end, to_far, to_mid, gram))
    rest_sibling = swap(jnp.where(middle, to_mid[1], to_far[1]))
    scores = weigh_call(
        place,
        (r_own, to_mid),
        (to_end, to_far),
        (first_sibling, rest_sibling),
        example_weights[None, :],
    )
    return gram[None], scores


def solution(mesh):
    placed = (
        P(("grp", "ex"), "feat"),
        P(("grp", "feat"), "ex"),
        P(("grp", "ex")),
        P(("grp", "feat"), None, None),
    )

    line = mesh.shape["ex"] == 4 and mesh.shape["feat"] == 4
    return jax.shard_map(
        local_line if line else local_any,
        mesh=mesh,
        in_specs=placed,
        out_specs=(P(("grp", "feat"), "ex", None, None), P(("grp", "feat"), "ex")),
        check_vma=False,
    )
```

```python
import math

import jax
import jax.numpy as jnp
from jax import lax
from jax.experimental import pallas as pl
from jax.experimental.pallas import tpu as pltpu
from jax.sharding import PartitionSpec as P

B = 128


def select_blocks(blocks3, indices):
    block_ids = lax.broadcasted_iota(jnp.int32, (indices.shape[0], blocks3.shape[1]), 1)
    onehot = (indices[:, None] == block_ids).astype(jnp.bfloat16)
    chosen = jnp.einsum("tnb,gn->tgb", blocks3, onehot, preferred_element_type=jnp.float32)
    return chosen.astype(jnp.bfloat16)


def tile_terms(blocks3, subset):
    group_size = math.gcd(subset.shape[0], 8)
    groups = subset.reshape(-1, group_size, 2)

    def group_tiles(group):
        left_block = select_blocks(blocks3, group[:, 0])
        right_block = select_blocks(blocks3, group[:, 1])
        product = jnp.einsum(
            "tsi,tsj->sij", left_block, right_block, preferred_element_type=jnp.float32
        )
        return jnp.where((group[:, 0] >= 0)[:, None, None], product, jnp.float32(0.0))

    return lax.map(group_tiles, groups).reshape(-1, blocks3.shape[2], blocks3.shape[2])


def local_any(slab_grads, query_grads, example_weights, tile_owner):
    tile_table = tile_owner[0]
    tok_count = slab_grads.shape[0]
    slab_full = lax.all_gather(slab_grads, "feat", axis=1, tiled=True)
    blocks3 = slab_full.reshape(tok_count, slab_full.shape[1] // B, B)
    row_total = tok_count * lax.axis_size("ex")
    summed = lax.psum_scatter(
        tile_terms(blocks3, tile_table).astype(jnp.bfloat16), "ex", scatter_dimension=0, tiled=True
    ).astype(jnp.float32)
    gram = (summed / row_total)[None]
    summed = lax.dot_general(
        lax.all_gather(query_grads, "ex", axis=1, tiled=True),
        slab_full,
        (((1,), (1,)), ((), ())),
        preferred_element_type=jnp.float32,
    )
    scores = summed * example_weights[None, :]
    return (gram, scores)


PAIR = ((0, 1), (1, 0), (2, 3), (3, 2))
INNER = ((1, 2), (2, 1))
TO_END = ((1, 0), (2, 3))
TO_MID = ((0, 1), (3, 2))
END_TO_FAR_MID = ((0, 2), (3, 1))
MID_TO_FAR_END = ((1, 3), (2, 0))
CORE = ((0, 1), (1, 0), (2, 3), (3, 2))
ACROSS = ((0, 2), (2, 0), (1, 3), (3, 1))


def plan(batches, own_count):
    out = []
    for sides in batches:
        for side in range(2):
            at = own_count
            for given, start, count, *flip in sides[side]:
                for plane, array in zip((1, 0), given) if isinstance(given, tuple) else [(2, given)]:
                    wide = array.shape[1]
                    if any(flip):
                        out.append((array, start, count, side, at, 0, wide // 2, wide // 2, plane))
                        out.append((array, start, count, side, at, wide // 2, 0, wide // 2, plane))
                    else:
                        out.append((array, start, count, side, at, 0, 0, wide, plane))
                at += count
    return out


def rows_of(batches):
    return sum(entry[2] for sides in batches[:1] for entry in sides[0])


def tile_call(place, table, always, carried=(), carried_sibling=None, part="both", scores=None):
    tiles = table.shape[0]
    moves = [plan([always], 0)]
    arrays = []
    for some in moves:
        for array, *_ in some:
            if not any(array is x for x in arrays):
                arrays.append(array)
    where = [[next(i for i, x in enumerate(arrays) if x is m[0]) for m in some] for some in moves]
    n = len(arrays)
    n_moves = sum(len(some) for some in moves)
    wide = arrays[0].shape[1]
    total = rows_of([always])
    half = tiles // 2
    per = wide // B
    extra = [] if carried_sibling is None else [carried_sibling]
    carried = list(carried) + extra
    n_own = len(carried) - len(extra)
    unroll = max(u for u in range(1, 22) if half // 2 % u == 0)
    n_out = 2 if part == "both" else 1
    inside = part == "both"

    n_scores = len(scores.count) if scores else 0
    score_arrays = scores.arrays if scores else []
    n_in = n + len(carried) + len(score_arrays)

    def kernel(place_ref, table_ref, *refs):
        score_sources = refs[n + len(carried) : n_in]
        score_outs = refs[n_in + n_out : n_in + n_out + n_scores]
        refs = refs[: n + len(carried)] + refs[n_in : n_in + n_out] + refs[n_in + n_out + n_scores :]
        if scores:
            score_scratch, refs = refs[-3:], refs[:-3]
            score_copies = scores.copies(score_sources, *score_scratch)
        row_refs = refs[:n]
        carried_refs = refs[n : n + len(carried)]
        out_refs = refs[n + len(carried) : n + len(carried) + n_out]
        outs = out_refs if inside else refs[n + len(carried) + n_out : -3]
        held = carried_refs
        rows, turned, sems = refs[-3:]
        parts = []
        for i in range(0 if inside else n_out):
            for j in range(2):
                some = pl.ds(j * (half // 2), half // 2)
                sem = sems.at[n_moves + len(carried) + 2 * i + j]
                parts.append(pltpu.make_async_copy(outs[i].at[some], out_refs[i].at[some], sem))
        copies = [[], [], []]
        at = 0
        for i, some in enumerate(moves):
            for (_, start, count, side, to, left, right, columns, plane), index in zip(some, where[i]):
                source = row_refs[index].at[pl.ds(start, count), pl.ds(left, columns)]
                into = rows.at[side, pl.ds(to, count), pl.ds(right, columns)]
                copies[plane].append(pltpu.make_async_copy(source, into, sems.at[at]))
                at += 1

        def each(some, do):
            for copy in some:
                do(copy)

        def rows_do(do):
            each(copies[2], do)
            for plane in range(2):
                if copies[plane]:
                    pl.when(place_ref[0] == plane)(lambda plane=plane: each(copies[plane], do))

        rows_do(lambda copy: copy.start())
        if scores:
            pl.when(place_ref[0] == 1)(lambda: each(score_copies, lambda copy: copy.start()))
        rows_do(lambda copy: copy.wait())

        for block in range(2 * per):
            side, column = divmod(block * B, wide)
            turned[block] = rows[side, :, column : column + B].T

        def product(tile):
            right = table_ref[tile, 1]
            return jnp.dot(
                turned[table_ref[tile, 0]],
                rows[right // per, :, pl.ds(pl.multiple_of((right % per) * B, B), B)],
                preferred_element_type=jnp.float32,
            )

        def sibling(tile, _):
            sum_ = product(tile)
            for ref in held[n_own:]:
                sum_ += ref[tile].astype(jnp.float32)
            outs[0][tile] = sum_.astype(outs[0].dtype)
            return 0

        def mine(tile, _):
            sum_ = product(tile + half)
            for ref in held[:n_own]:
                sum_ += ref[tile].astype(jnp.float32)
            if part == "own":
                scale = 1.0 / place_ref[7].astype(jnp.float32)
                sum_ = sum_ * jnp.where(table_ref[tile + half, 2] == 1, scale, 0.0)
            outs[-1][tile] = sum_
            return 0

        if part != "own":
            for j in range(2):
                lax.fori_loop(j * (half // 2), (j + 1) * (half // 2), sibling, 0, unroll=unroll)
                if parts:
                    parts[j].start()
        if part != "sibling":
            for j in range(2):
                lax.fori_loop(j * (half // 2), (j + 1) * (half // 2), mine, 0, unroll=unroll)
                if parts:
                    parts[j - 2].start()
        if scores:

            @pl.when(place_ref[0] == 1)
            def _():
                scores.compute(place_ref, score_outs, *score_scratch[:2], score_copies)

        for copy in parts:
            copy.wait()

    smem = pl.BlockSpec(memory_space=pltpu.SMEM)
    hbm = pl.BlockSpec(memory_space=pltpu.HBM)
    vmem = pl.BlockSpec(memory_space=pltpu.VMEM)
    outs = []
    if part != "own":
        outs.append(jax.ShapeDtypeStruct((half, B, B), jnp.bfloat16))
    if part != "sibling":
        outs.append(jax.ShapeDtypeStruct((half, B, B), jnp.float32))
    return pl.pallas_call(
        kernel,
        out_shape=outs + (scores.out_shape if scores else []),
        in_specs=[smem, smem] + [hbm] * n + [vmem] * len(carried) + [hbm] * len(score_arrays),
        out_specs=[vmem if inside else hbm] * n_out + [pl.BlockSpec(memory_space=pltpu.VMEM)] * n_scores,
        scratch_shapes=[pltpu.VMEM(x.shape, x.dtype) for x in outs if not inside]
        + [
            pltpu.VMEM((2, total, wide), jnp.bfloat16),
            pltpu.VMEM((2 * per, B, total), jnp.bfloat16),
            pltpu.SemaphoreType.DMA((n_moves + len(carried) + 2 * n_out,)),
        ]
        + (scores.scratch if scores else []),
        compiler_params=pltpu.CompilerParams(vmem_limit_bytes=13 * 2**20),
        cost_estimate=pl.CostEstimate(flops=0, bytes_accessed=0, transcendentals=0),
    )(place, table, *arrays, *carried, *score_arrays)


class Scores:
    def __init__(self, parts, slots):
        self.count = [rows_of([slot]) for slot in slots]
        self.moves = []
        for i, slot in enumerate(slots):
            self.moves += plan([slot], sum(self.count[:i]))
        self.quarter = parts[0][0].shape[1]
        lengths = [pair[0].shape[0] for pair in parts]
        self.queries = [x for pair in parts for x in pair]
        self.wide = self.moves[0][0].shape[1]
        self.group = sum(lengths) // 4
        self.arrays = [move[0] for move in self.moves]
        self.out_shape = [
            jax.ShapeDtypeStruct((2, self.group, c), jnp.bfloat16) for c in self.count
        ]
        self.scratch = [
            pltpu.VMEM((2, sum(self.count), self.wide), jnp.bfloat16),
            pltpu.SemaphoreType.DMA((len(self.moves),)),
        ]

    def copies(self, sources, rows, sems):
        out = []
        for i, (_, start, count, side, to, *_) in enumerate(self.moves):
            into = rows.at[side, pl.ds(to, count)]
            out.append(pltpu.make_async_copy(sources[i].at[pl.ds(start, count)], into, sems.at[i]))
        return out

    def compute(self, place_ref, outs, rows, query, copies):
        group, quarter = self.group, self.quarter
        per = self.wide // quarter
        for i, out in enumerate(outs):
            first = sum(self.count[:i])
            for copy, move in zip(copies, self.moves):
                if move[3] < 2 and first <= move[4] < first + self.count[i]:
                    copy.wait()
            for j in range(2):
                total = None
                for k in range(4):
                    spot = place_ref[1 + k]
                    columns = pl.ds(pl.multiple_of((spot % per) * quarter, quarter), quarter)
                    term = lax.dot_general(
                        query[2 * k + j][...],
                        rows[spot // per, first : first + self.count[i], columns],
                        (((1,), (1,)), ((), ())),
                        preferred_element_type=jnp.float32,
                    )
                    total = term if total is None else total + term
                out[j] = total.astype(out.dtype)


def score_call(place, parts, slots):
    scores = Scores(parts, slots)
    n, m = len(slots), len(scores.moves)

    def kernel(place_ref, *refs):
        outs = refs[m + 8 : m + 8 + n]
        rows, sems = refs[m + 8 + n :]

        @pl.when(place_ref[0] == 1)
        def _():
            copies = scores.copies(refs[:m], rows, sems)
            for copy in copies:
                copy.start()
            scores.compute(place_ref, outs, rows, refs[m : m + 8], copies)

    smem = pl.BlockSpec(memory_space=pltpu.SMEM)
    hbm = pl.BlockSpec(memory_space=pltpu.HBM)
    vmem = pl.BlockSpec(memory_space=pltpu.VMEM)
    return pl.pallas_call(
        kernel,
        out_shape=scores.out_shape,
        in_specs=[smem] + [hbm] * m + [vmem] * 8,
        out_specs=[vmem] * n,
        scratch_shapes=scores.scratch,
        compiler_params=pltpu.CompilerParams(vmem_limit_bytes=9 * 2**20),
        cost_estimate=pl.CostEstimate(flops=0, bytes_accessed=0, transcendentals=0),
    )(place, *scores.arrays, *scores.queries)


def weigh_call(place, on_middle, on_ends, swapped, weights):
    group, count = swapped[0].shape

    def kernel(place_ref, *refs):
        late, core = place_ref[5], place_ref[6]
        weight, out = refs[6], refs[7]

        def put(i, block, own_rows):
            row = late if i == 0 else 1 - late
            column = core if own_rows else 1 - core
            across = pl.ds(pl.multiple_of(column * count, count), count)
            down = pl.ds(pl.multiple_of(row * group, group), group)
            out[down, across] = block.astype(jnp.float32) * weight[:, across]

        for i in range(2):
            pl.when(place_ref[0] == 1)(lambda i=i: put(i, refs[i][0], True))
            pl.when(place_ref[0] == 0)(lambda i=i: put(i, refs[2 + i][0], True))
            put(i, refs[4 + i][...], False)

    smem = pl.BlockSpec(memory_space=pltpu.SMEM)
    vmem = pl.BlockSpec(memory_space=pltpu.VMEM)
    return pl.pallas_call(
        kernel,
        out_shape=jax.ShapeDtypeStruct((2 * group, 2 * count), jnp.float32),
        in_specs=[smem] + [vmem] * 7,
        out_specs=vmem,
        compiler_params=pltpu.CompilerParams(vmem_limit_bytes=8 * 2**20),
        cost_estimate=pl.CostEstimate(flops=0, bytes_accessed=0, transcendentals=0),
    )(place, *on_middle, *on_ends, *swapped, weights)


def after(values, *done):
    return lax.optimization_barrier(tuple(values) + done)[: len(values)]


def local_line(slab_grads, query_grads, example_weights, tile_owner):
    count, quarter = slab_grads.shape
    half, piece = count // 2, count // 4
    e = lax.axis_index("ex")
    f = lax.axis_index("feat")
    core = f % 2
    middle = jnp.logical_or(e == 1, e == 2)
    late = (e >= 2).astype(jnp.int32)

    def move(value, pairs):
        return lax.ppermute(value, "ex", pairs)

    def across(value):
        return lax.ppermute(value, "feat", ACROSS)

    def swap(value):
        return lax.ppermute(value, "feat", CORE)

    def across_on(value, which):
        pairs = [(p * 4 + g, p * 4 + (g ^ 2)) for p in which for g in range(4)]
        return lax.ppermute(value, ("ex", "feat"), pairs)

    def swap_on(value, which):
        pairs = [(p * 4 + g, p * 4 + (g ^ 1)) for p in which for g in range(4)]
        return lax.ppermute(value, ("ex", "feat"), pairs)

    mids, ends = (1, 2), (0, 3)

    def whole(a, b):
        return ([(a, 0, half)], [(b, 0, half)])

    slots = tile_owner.shape[1] // 4
    own_tiles = lax.dynamic_slice(tile_owner[0], (e * slots, 0), (slots, 2))
    tiles = jnp.concatenate([swap(own_tiles), own_tiles], axis=0)
    blocks = quarter // B
    valid = (tiles[:, :1] >= 0).astype(jnp.int32)
    tiles = jnp.maximum(tiles, 0)
    table = ((tiles // blocks) ^ f) * blocks + tiles % blocks
    table = jnp.concatenate([table, valid], axis=1)
    order = jnp.where(e == 2, jnp.array([2, 3, 1, 0]), jnp.array([1, 0, 2, 3])).astype(jnp.int32)
    place = jnp.concatenate(
        [
            middle.astype(jnp.int32)[None],
            order ^ f,
            late[None],
            core[None],
            jnp.array([4 * count], jnp.int32),
        ]
    )

    give = lax.dynamic_slice(slab_grads, ((1 - core) * half, 0), (half, quarter))
    (slab_grads,) = after((slab_grads,), give)
    keep = lax.dynamic_slice(slab_grads, (core * half, 0), (half, quarter))
    own = jnp.concatenate([keep, swap(give)], axis=1)
    q_half = query_grads.shape[0] // 2

    own_x = across(own)
    near = move(own, PAIR)
    inner = move(own, INNER)

    def halves(value, which):
        return lax.dynamic_slice(value, (which * q_half, 0), (q_half, quarter))

    q_mine, q_other = halves(query_grads, late), halves(query_grads, 1 - late)
    q_mine_sibling = swap(q_mine)
    near, inner, own, own_x, q_mine, q_other, table, q_mine_sibling = after(
        (near, inner, own, own_x, q_mine, q_other, table, q_mine_sibling)
    )
    near_x = across(near)
    outer = move(near, INNER)
    inner_end = move(inner, TO_END)
    q_end_other = move(q_other, TO_MID)
    sibling0, sum0 = tile_call(place, table, whole(own, own_x))

    inner, inner_end, outer, near, near_x, q_end_other, q_mine, sibling0, sum0 = after(
        (inner, inner_end, outer, near, near_x, q_end_other, q_mine, sibling0, sum0)
    )
    second = jnp.where(middle, outer, inner_end)
    second_x = across(second)
    outer_end = move(outer, TO_END)
    q_inner = move(q_other, INNER)
    q_far = move(q_end_other, INNER)
    q_end = move(q_mine, TO_MID)
    sibling1, sum1 = tile_call(place, table, whole(near, near_x), [sum0], sibling0)

    second, second_x, outer_end, inner, sum1, sibling1 = after(
        (second, second_x, outer_end, inner, sum1, sibling1)
    )
    third = jnp.where(middle, inner, outer_end)
    third_x = across(third)
    parts = [(q_mine, q_mine_sibling)] + [(x, swap(x)) for x in (q_end, q_inner, q_far)]
    slots3 = [whole(own, own_x), whole(near, near_x), whole(second, second_x)]
    r_own, r_near, r_outer = score_call(place, parts, slots3)
    far = move(r_outer, INNER)
    to_end = move(r_near, TO_END)
    sibling2, sum2 = tile_call(place, table, whole(second, second_x), [sum1], sibling1)
    third_sibling = swap(third)

    first = jnp.where(middle, r_own[1], to_end[1])
    third_x, to_end, far, sibling2, first = after((third_x, to_end, far, sibling2, first), sum2, r_own)
    first_sibling = swap(first)
    third_x_sibling = swap(third_x)
    (r_inner,) = score_call(place, parts, [whole(third, third_x)])
    sibling2 = swap(sibling2)
    r_inner, far = after((r_inner, far))
    to_far = move(far, TO_END)
    to_mid = move(r_inner, INNER)
    (gram,) = tile_call(
        place,
        table,
        (
            [(third, 0, half), (third_sibling, 0, half, True)],
            [(third_x, 0, half), (third_x_sibling, 0, half, True)],
        ),
        [sum2, sibling2],
        part="own",
    )
    to_end, to_far, to_mid, gram = after((to_end, to_far, to_mid, gram))
    rest_sibling = swap(jnp.where(middle, to_mid[1], to_far[1]))
    scores = weigh_call(
        place,
        (r_own, to_mid),
        (to_end, to_far),
        (first_sibling, rest_sibling),
        example_weights[None, :],
    )
    return gram[None], scores


def solution(mesh):
    placed = (
        P(("grp", "ex"), "feat"),
        P(("grp", "feat"), "ex"),
        P(("grp", "ex")),
        P(("grp", "feat"), None, None),
    )

    line = mesh.shape["ex"] == 4 and mesh.shape["feat"] == 4
    return jax.shard_map(
        local_line if line else local_any,
        mesh=mesh,
        in_specs=placed,
        out_specs=(P(("grp", "feat"), "ex", None, None), P(("grp", "feat"), "ex")),
        check_vma=False,
    )
```

```python
import math

import jax
import jax.numpy as jnp
from jax import lax
from jax.experimental import pallas as pl
from jax.experimental.pallas import tpu as pltpu
from jax.sharding import PartitionSpec as P

B = 128


def select_blocks(blocks3, indices):
    block_ids = lax.broadcasted_iota(jnp.int32, (indices.shape[0], blocks3.shape[1]), 1)
    onehot = (indices[:, None] == block_ids).astype(jnp.bfloat16)
    chosen = jnp.einsum("tnb,gn->tgb", blocks3, onehot, preferred_element_type=jnp.float32)
    return chosen.astype(jnp.bfloat16)


def tile_terms(blocks3, subset):
    group_size = math.gcd(subset.shape[0], 8)
    groups = subset.reshape(-1, group_size, 2)

    def group_tiles(group):
        left_block = select_blocks(blocks3, group[:, 0])
        right_block = select_blocks(blocks3, group[:, 1])
        product = jnp.einsum(
            "tsi,tsj->sij", left_block, right_block, preferred_element_type=jnp.float32
        )
        return jnp.where((group[:, 0] >= 0)[:, None, None], product, jnp.float32(0.0))

    return lax.map(group_tiles, groups).reshape(-1, blocks3.shape[2], blocks3.shape[2])


def local_any(slab_grads, query_grads, example_weights, tile_owner):
    tile_table = tile_owner[0]
    tok_count = slab_grads.shape[0]
    slab_full = lax.all_gather(slab_grads, "feat", axis=1, tiled=True)
    blocks3 = slab_full.reshape(tok_count, slab_full.shape[1] // B, B)
    row_total = tok_count * lax.axis_size("ex")
    summed = lax.psum_scatter(
        tile_terms(blocks3, tile_table).astype(jnp.bfloat16), "ex", scatter_dimension=0, tiled=True
    ).astype(jnp.float32)
    gram = (summed / row_total)[None]
    summed = lax.dot_general(
        lax.all_gather(query_grads, "ex", axis=1, tiled=True),
        slab_full,
        (((1,), (1,)), ((), ())),
        preferred_element_type=jnp.float32,
    )
    scores = summed * example_weights[None, :]
    return (gram, scores)


PAIR = ((0, 1), (1, 0), (2, 3), (3, 2))
INNER = ((1, 2), (2, 1))
TO_END = ((1, 0), (2, 3))
TO_MID = ((0, 1), (3, 2))
END_TO_FAR_MID = ((0, 2), (3, 1))
MID_TO_FAR_END = ((1, 3), (2, 0))
CORE = ((0, 1), (1, 0), (2, 3), (3, 2))
ACROSS = ((0, 2), (2, 0), (1, 3), (3, 1))


def plan(batches, own_count):
    out = []
    for sides in batches:
        for side in range(2):
            at = own_count
            for given, start, count, *flip in sides[side]:
                for plane, array in zip((1, 0), given) if isinstance(given, tuple) else [(2, given)]:
                    wide = array.shape[1]
                    if any(flip):
                        out.append((array, start, count, side, at, 0, wide // 2, wide // 2, plane))
                        out.append((array, start, count, side, at, wide // 2, 0, wide // 2, plane))
                    else:
                        out.append((array, start, count, side, at, 0, 0, wide, plane))
                at += count
    return out


def rows_of(batches):
    return sum(entry[2] for sides in batches[:1] for entry in sides[0])


def tile_call(place, table, always, carried=(), carried_sibling=None, part="both", scores=None):
    tiles = table.shape[0]
    moves = [plan([always], 0)]
    arrays = []
    for some in moves:
        for array, *_ in some:
            if not any(array is x for x in arrays):
                arrays.append(array)
    where = [[next(i for i, x in enumerate(arrays) if x is m[0]) for m in some] for some in moves]
    n = len(arrays)
    n_moves = sum(len(some) for some in moves)
    wide = arrays[0].shape[1]
    total = rows_of([always])
    half = tiles // 2
    per = wide // B
    extra = [] if carried_sibling is None else [carried_sibling]
    carried = list(carried) + extra
    n_own = len(carried) - len(extra)
    unroll = max(u for u in range(1, 22) if half // 2 % u == 0)
    n_out = 2 if part == "both" else 1
    inside = part == "both"

    n_scores = len(scores.count) if scores else 0
    score_arrays = scores.arrays if scores else []
    n_in = n + len(carried) + len(score_arrays)

    def kernel(place_ref, table_ref, *refs):
        score_sources = refs[n + len(carried) : n_in]
        score_outs = refs[n_in + n_out : n_in + n_out + n_scores]
        refs = refs[: n + len(carried)] + refs[n_in : n_in + n_out] + refs[n_in + n_out + n_scores :]
        if scores:
            score_scratch, refs = refs[-3:], refs[:-3]
            score_copies = scores.copies(score_sources, *score_scratch)
        row_refs = refs[:n]
        carried_refs = refs[n : n + len(carried)]
        out_refs = refs[n + len(carried) : n + len(carried) + n_out]
        outs = out_refs if inside else refs[n + len(carried) + n_out : -3]
        held = carried_refs
        rows, turned, sems = refs[-3:]
        parts = []
        for i in range(0 if inside else n_out):
            for j in range(2):
                some = pl.ds(j * (half // 2), half // 2)
                sem = sems.at[n_moves + len(carried) + 2 * i + j]
                parts.append(pltpu.make_async_copy(outs[i].at[some], out_refs[i].at[some], sem))
        copies = [[], [], []]
        at = 0
        for i, some in enumerate(moves):
            for (_, start, count, side, to, left, right, columns, plane), index in zip(some, where[i]):
                source = row_refs[index].at[pl.ds(start, count), pl.ds(left, columns)]
                into = rows.at[side, pl.ds(to, count), pl.ds(right, columns)]
                copies[plane].append(pltpu.make_async_copy(source, into, sems.at[at]))
                at += 1

        def each(some, do):
            for copy in some:
                do(copy)

        def rows_do(do):
            each(copies[2], do)
            for plane in range(2):
                if copies[plane]:
                    pl.when(place_ref[0] == plane)(lambda plane=plane: each(copies[plane], do))

        rows_do(lambda copy: copy.start())
        if scores:
            pl.when(place_ref[0] == 1)(lambda: each(score_copies, lambda copy: copy.start()))
        rows_do(lambda copy: copy.wait())

        for block in range(2 * per):
            side, column = divmod(block * B, wide)
            turned[block] = rows[side, :, column : column + B].T

        def product(tile):
            right = table_ref[tile, 1]
            return jnp.dot(
                turned[table_ref[tile, 0]],
                rows[right // per, :, pl.ds(pl.multiple_of((right % per) * B, B), B)],
                preferred_element_type=jnp.float32,
            )

        def sibling(tile, _):
            sum_ = product(tile)
            for ref in held[n_own:]:
                sum_ += ref[tile].astype(jnp.float32)
            outs[0][tile] = sum_.astype(outs[0].dtype)
            return 0

        def mine(tile, _):
            sum_ = product(tile + half)
            for ref in held[:n_own]:
                sum_ += ref[tile].astype(jnp.float32)
            if part == "own":
                scale = 1.0 / place_ref[7].astype(jnp.float32)
                sum_ = sum_ * jnp.where(table_ref[tile + half, 2] == 1, scale, 0.0)
            outs[-1][tile] = sum_
            return 0

        if part != "own":
            for j in range(2):
                lax.fori_loop(j * (half // 2), (j + 1) * (half // 2), sibling, 0, unroll=unroll)
                if parts:
                    parts[j].start()
        if part != "sibling":
            for j in range(2):
                lax.fori_loop(j * (half // 2), (j + 1) * (half // 2), mine, 0, unroll=unroll)
                if parts:
                    parts[j - 2].start()
        if scores:

            @pl.when(place_ref[0] == 1)
            def _():
                scores.compute(place_ref, score_outs, *score_scratch[:2], score_copies)

        for copy in parts:
            copy.wait()

    smem = pl.BlockSpec(memory_space=pltpu.SMEM)
    hbm = pl.BlockSpec(memory_space=pltpu.HBM)
    vmem = pl.BlockSpec(memory_space=pltpu.VMEM)
    outs = []
    if part != "own":
        outs.append(jax.ShapeDtypeStruct((half, B, B), jnp.bfloat16))
    if part != "sibling":
        outs.append(jax.ShapeDtypeStruct((half, B, B), jnp.float32))
    return pl.pallas_call(
        kernel,
        out_shape=outs + (scores.out_shape if scores else []),
        in_specs=[smem, smem] + [hbm] * n + [vmem] * len(carried) + [hbm] * len(score_arrays),
        out_specs=[vmem if inside else hbm] * n_out + [pl.BlockSpec(memory_space=pltpu.VMEM)] * n_scores,
        scratch_shapes=[pltpu.VMEM(x.shape, x.dtype) for x in outs if not inside]
        + [
            pltpu.VMEM((2, total, wide), jnp.bfloat16),
            pltpu.VMEM((2 * per, B, total), jnp.bfloat16),
            pltpu.SemaphoreType.DMA((n_moves + len(carried) + 2 * n_out,)),
        ]
        + (scores.scratch if scores else []),
        compiler_params=pltpu.CompilerParams(vmem_limit_bytes=13 * 2**20),
        cost_estimate=pl.CostEstimate(flops=0, bytes_accessed=0, transcendentals=0),
    )(place, table, *arrays, *carried, *score_arrays)


class Scores:
    def __init__(self, parts, slots):
        self.count = [rows_of([slot]) for slot in slots]
        self.moves = []
        for i, slot in enumerate(slots):
            self.moves += plan([slot], sum(self.count[:i]))
        self.quarter = parts[0][0].shape[1]
        lengths = [pair[0].shape[0] for pair in parts]
        self.queries = [x for pair in parts for x in pair]
        self.wide = self.moves[0][0].shape[1]
        self.group = sum(lengths) // 4
        self.arrays = [move[0] for move in self.moves]
        self.out_shape = [
            jax.ShapeDtypeStruct((2, self.group, c), jnp.bfloat16) for c in self.count
        ]
        self.scratch = [
            pltpu.VMEM((2, sum(self.count), self.wide), jnp.bfloat16),
            pltpu.SemaphoreType.DMA((len(self.moves),)),
        ]

    def copies(self, sources, rows, sems):
        out = []
        for i, (_, start, count, side, to, *_) in enumerate(self.moves):
            into = rows.at[side, pl.ds(to, count)]
            out.append(pltpu.make_async_copy(sources[i].at[pl.ds(start, count)], into, sems.at[i]))
        return out

    def compute(self, place_ref, outs, rows, query, copies):
        group, quarter = self.group, self.quarter
        per = self.wide // quarter
        for i, out in enumerate(outs):
            first = sum(self.count[:i])
            for copy, move in zip(copies, self.moves):
                if move[3] < 2 and first <= move[4] < first + self.count[i]:
                    copy.wait()
            for j in range(2):
                total = None
                for k in range(4):
                    spot = place_ref[1 + k]
                    columns = pl.ds(pl.multiple_of((spot % per) * quarter, quarter), quarter)
                    term = lax.dot_general(
                        query[2 * k + j][...],
                        rows[spot // per, first : first + self.count[i], columns],
                        (((1,), (1,)), ((), ())),
                        preferred_element_type=jnp.float32,
                    )
                    total = term if total is None else total + term
                out[j] = total.astype(out.dtype)


def score_call(place, parts, slots):
    scores = Scores(parts, slots)
    n, m = len(slots), len(scores.moves)

    def kernel(place_ref, *refs):
        outs = refs[m + 8 : m + 8 + n]
        rows, sems = refs[m + 8 + n :]

        @pl.when(place_ref[0] == 1)
        def _():
            copies = scores.copies(refs[:m], rows, sems)
            for copy in copies:
                copy.start()
            scores.compute(place_ref, outs, rows, refs[m : m + 8], copies)

    smem = pl.BlockSpec(memory_space=pltpu.SMEM)
    hbm = pl.BlockSpec(memory_space=pltpu.HBM)
    vmem = pl.BlockSpec(memory_space=pltpu.VMEM)
    return pl.pallas_call(
        kernel,
        out_shape=scores.out_shape,
        in_specs=[smem] + [hbm] * m + [vmem] * 8,
        out_specs=[vmem] * n,
        scratch_shapes=scores.scratch,
        compiler_params=pltpu.CompilerParams(vmem_limit_bytes=9 * 2**20),
        cost_estimate=pl.CostEstimate(flops=0, bytes_accessed=0, transcendentals=0),
    )(place, *scores.arrays, *scores.queries)


def weigh_call(place, on_middle, on_ends, swapped, weights):
    group, count = swapped[0].shape

    def kernel(place_ref, *refs):
        late, core = place_ref[5], place_ref[6]
        weight, out = refs[6], refs[7]

        def put(i, block, own_rows):
            row = late if i == 0 else 1 - late
            column = core if own_rows else 1 - core
            across = pl.ds(pl.multiple_of(column * count, count), count)
            down = pl.ds(pl.multiple_of(row * group, group), group)
            out[down, across] = block.astype(jnp.float32) * weight[:, across]

        for i in range(2):
            pl.when(place_ref[0] == 1)(lambda i=i: put(i, refs[i][0], True))
            pl.when(place_ref[0] == 0)(lambda i=i: put(i, refs[2 + i][0], True))
            put(i, refs[4 + i][...], False)

    smem = pl.BlockSpec(memory_space=pltpu.SMEM)
    vmem = pl.BlockSpec(memory_space=pltpu.VMEM)
    return pl.pallas_call(
        kernel,
        out_shape=jax.ShapeDtypeStruct((2 * group, 2 * count), jnp.float32),
        in_specs=[smem] + [vmem] * 7,
        out_specs=vmem,
        compiler_params=pltpu.CompilerParams(vmem_limit_bytes=8 * 2**20),
        cost_estimate=pl.CostEstimate(flops=0, bytes_accessed=0, transcendentals=0),
    )(place, *on_middle, *on_ends, *swapped, weights)


def after(values, *done):
    return lax.optimization_barrier(tuple(values) + done)[: len(values)]


def local_line(slab_grads, query_grads, example_weights, tile_owner):
    count, quarter = slab_grads.shape
    half, piece = count // 2, count // 4
    e = lax.axis_index("ex")
    f = lax.axis_index("feat")
    core = f % 2
    middle = jnp.logical_or(e == 1, e == 2)
    late = (e >= 2).astype(jnp.int32)

    def move(value, pairs):
        return lax.ppermute(value, "ex", pairs)

    def across(value):
        return lax.ppermute(value, "feat", ACROSS)

    def swap(value):
        return lax.ppermute(value, "feat", CORE)

    def across_on(value, which):
        pairs = [(p * 4 + g, p * 4 + (g ^ 2)) for p in which for g in range(4)]
        return lax.ppermute(value, ("ex", "feat"), pairs)

    def swap_on(value, which):
        pairs = [(p * 4 + g, p * 4 + (g ^ 1)) for p in which for g in range(4)]
        return lax.ppermute(value, ("ex", "feat"), pairs)

    mids, ends = (1, 2), (0, 3)

    def whole(a, b):
        return ([(a, 0, half)], [(b, 0, half)])

    slots = tile_owner.shape[1] // 4
    own_tiles = lax.dynamic_slice(tile_owner[0], (e * slots, 0), (slots, 2))
    tiles = jnp.concatenate([swap(own_tiles), own_tiles], axis=0)
    blocks = quarter // B
    valid = (tiles[:, :1] >= 0).astype(jnp.int32)
    tiles = jnp.maximum(tiles, 0)
    table = ((tiles // blocks) ^ f) * blocks + tiles % blocks
    table = jnp.concatenate([table, valid], axis=1)
    order = jnp.where(e == 2, jnp.array([2, 3, 1, 0]), jnp.array([1, 0, 2, 3])).astype(jnp.int32)
    place = jnp.concatenate(
        [
            middle.astype(jnp.int32)[None],
            order ^ f,
            late[None],
            core[None],
            jnp.array([4 * count], jnp.int32),
        ]
    )

    give = lax.dynamic_slice(slab_grads, ((1 - core) * half, 0), (half, quarter))
    (slab_grads,) = after((slab_grads,), give)
    keep = lax.dynamic_slice(slab_grads, (core * half, 0), (half, quarter))
    own = jnp.concatenate([keep, swap(give)], axis=1)
    q_half = query_grads.shape[0] // 2

    own_x = across(own)
    near = move(own, PAIR)
    inner = move(own, INNER)

    def halves(value, which):
        return lax.dynamic_slice(value, (which * q_half, 0), (q_half, quarter))

    q_mine, q_other = halves(query_grads, late), halves(query_grads, 1 - late)
    q_mine_sibling = swap(q_mine)
    near, inner, own, own_x, q_mine, q_other, table, q_mine_sibling = after(
        (near, inner, own, own_x, q_mine, q_other, table, q_mine_sibling)
    )
    near_x = across(near)
    outer = move(near, INNER)
    inner_end = move(inner, TO_END)
    q_end_other = move(q_other, TO_MID)
    sibling0, sum0 = tile_call(place, table, whole(own, own_x))

    inner, inner_end, outer, near, near_x, q_end_other, q_mine, sibling0, sum0 = after(
        (inner, inner_end, outer, near, near_x, q_end_other, q_mine, sibling0, sum0)
    )
    second = jnp.where(middle, outer, inner_end)
    second_x = across(second)
    outer_end = move(outer, TO_END)
    q_inner = move(q_other, INNER)
    q_far = move(q_end_other, INNER)
    sibling1, sum1 = tile_call(place, table, whole(near, near_x), [sum0], sibling0)
    (q_late,) = after((q_mine,), sum1)
    q_end = move(q_late, TO_MID)

    second, second_x, outer_end, inner, sum1, sibling1 = after(
        (second, second_x, outer_end, inner, sum1, sibling1)
    )
    third = jnp.where(middle, inner, outer_end)
    third_x = across(third)
    parts = [(q_mine, q_mine_sibling)] + [(x, swap(x)) for x in (q_end, q_inner, q_far)]
    slots3 = [whole(own, own_x), whole(near, near_x), whole(second, second_x)]
    r_own, r_near, r_outer = score_call(place, parts, slots3)
    far = move(r_outer, INNER)
    to_end = move(r_near, TO_END)
    sibling2, sum2 = tile_call(place, table, whole(second, second_x), [sum1], sibling1)
    third_sibling = swap(third)

    first = jnp.where(middle, r_own[1], to_end[1])
    third_x, to_end, far, sibling2, first = after((third_x, to_end, far, sibling2, first), sum2, r_own)
    first_sibling = swap(first)
    third_x_sibling = swap(third_x)
    (r_inner,) = score_call(place, parts, [whole(third, third_x)])
    sibling2 = swap(sibling2)
    r_inner, far = after((r_inner, far))
    to_far = move(far, TO_END)
    to_mid = move(r_inner, INNER)
    (gram,) = tile_call(
        place,
        table,
        (
            [(third, 0, half), (third_sibling, 0, half, True)],
            [(third_x, 0, half), (third_x_sibling, 0, half, True)],
        ),
        [sum2, sibling2],
        part="own",
    )
    to_end, to_far, to_mid, gram = after((to_end, to_far, to_mid, gram))
    rest_sibling = swap(jnp.where(middle, to_mid[1], to_far[1]))
    scores = weigh_call(
        place,
        (r_own, to_mid),
        (to_end, to_far),
        (first_sibling, rest_sibling),
        example_weights[None, :],
    )
    return gram[None], scores


def solution(mesh):
    placed = (
        P(("grp", "ex"), "feat"),
        P(("grp", "feat"), "ex"),
        P(("grp", "ex")),
        P(("grp", "feat"), None, None),
    )

    line = mesh.shape["ex"] == 4 and mesh.shape["feat"] == 4
    return jax.shard_map(
        local_line if line else local_any,
        mesh=mesh,
        in_specs=placed,
        out_specs=(P(("grp", "feat"), "ex", None, None), P(("grp", "feat"), "ex")),
        check_vma=False,
    )
```

```python
import math

import jax
import jax.numpy as jnp
from jax import lax
from jax.experimental import pallas as pl
from jax.experimental.pallas import tpu as pltpu
from jax.sharding import PartitionSpec as P

B = 128


def select_blocks(blocks3, indices):
    block_ids = lax.broadcasted_iota(jnp.int32, (indices.shape[0], blocks3.shape[1]), 1)
    onehot = (indices[:, None] == block_ids).astype(jnp.bfloat16)
    chosen = jnp.einsum("tnb,gn->tgb", blocks3, onehot, preferred_element_type=jnp.float32)
    return chosen.astype(jnp.bfloat16)


def tile_terms(blocks3, subset):
    group_size = math.gcd(subset.shape[0], 8)
    groups = subset.reshape(-1, group_size, 2)

    def group_tiles(group):
        left_block = select_blocks(blocks3, group[:, 0])
        right_block = select_blocks(blocks3, group[:, 1])
        product = jnp.einsum(
            "tsi,tsj->sij", left_block, right_block, preferred_element_type=jnp.float32
        )
        return jnp.where((group[:, 0] >= 0)[:, None, None], product, jnp.float32(0.0))

    return lax.map(group_tiles, groups).reshape(-1, blocks3.shape[2], blocks3.shape[2])


def local_any(slab_grads, query_grads, example_weights, tile_owner):
    tile_table = tile_owner[0]
    tok_count = slab_grads.shape[0]
    slab_full = lax.all_gather(slab_grads, "feat", axis=1, tiled=True)
    blocks3 = slab_full.reshape(tok_count, slab_full.shape[1] // B, B)
    row_total = tok_count * lax.axis_size("ex")
    summed = lax.psum_scatter(
        tile_terms(blocks3, tile_table).astype(jnp.bfloat16), "ex", scatter_dimension=0, tiled=True
    ).astype(jnp.float32)
    gram = (summed / row_total)[None]
    summed = lax.dot_general(
        lax.all_gather(query_grads, "ex", axis=1, tiled=True),
        slab_full,
        (((1,), (1,)), ((), ())),
        preferred_element_type=jnp.float32,
    )
    scores = summed * example_weights[None, :]
    return (gram, scores)


PAIR = ((0, 1), (1, 0), (2, 3), (3, 2))
INNER = ((1, 2), (2, 1))
TO_END = ((1, 0), (2, 3))
TO_MID = ((0, 1), (3, 2))
END_TO_FAR_MID = ((0, 2), (3, 1))
MID_TO_FAR_END = ((1, 3), (2, 0))
CORE = ((0, 1), (1, 0), (2, 3), (3, 2))
ACROSS = ((0, 2), (2, 0), (1, 3), (3, 1))


def plan(batches, own_count):
    out = []
    for sides in batches:
        for side in range(2):
            at = own_count
            for given, start, count, *flip in sides[side]:
                for plane, array in zip((1, 0), given) if isinstance(given, tuple) else [(2, given)]:
                    wide = array.shape[1]
                    if any(flip):
                        out.append((array, start, count, side, at, 0, wide // 2, wide // 2, plane))
                        out.append((array, start, count, side, at, wide // 2, 0, wide // 2, plane))
                    else:
                        out.append((array, start, count, side, at, 0, 0, wide, plane))
                at += count
    return out


def rows_of(batches):
    return sum(entry[2] for sides in batches[:1] for entry in sides[0])


def tile_call(place, table, always, carried=(), carried_sibling=None, part="both", scores=None):
    tiles = table.shape[0]
    moves = [plan([always], 0)]
    arrays = []
    for some in moves:
        for array, *_ in some:
            if not any(array is x for x in arrays):
                arrays.append(array)
    where = [[next(i for i, x in enumerate(arrays) if x is m[0]) for m in some] for some in moves]
    n = len(arrays)
    n_moves = sum(len(some) for some in moves)
    wide = arrays[0].shape[1]
    total = rows_of([always])
    half = tiles // 2
    per = wide // B
    extra = [] if carried_sibling is None else [carried_sibling]
    carried = list(carried) + extra
    n_own = len(carried) - len(extra)
    unroll = max(u for u in range(1, 22) if half // 2 % u == 0)
    n_out = 2 if part == "both" else 1
    inside = part == "both"

    n_scores = len(scores.count) if scores else 0
    score_arrays = scores.arrays if scores else []
    n_in = n + len(carried) + len(score_arrays)

    def kernel(place_ref, table_ref, *refs):
        score_sources = refs[n + len(carried) : n_in]
        score_outs = refs[n_in + n_out : n_in + n_out + n_scores]
        refs = refs[: n + len(carried)] + refs[n_in : n_in + n_out] + refs[n_in + n_out + n_scores :]
        if scores:
            score_scratch, refs = refs[-3:], refs[:-3]
            score_copies = scores.copies(score_sources, *score_scratch)
        row_refs = refs[:n]
        carried_refs = refs[n : n + len(carried)]
        out_refs = refs[n + len(carried) : n + len(carried) + n_out]
        outs = out_refs if inside else refs[n + len(carried) + n_out : -3]
        held = carried_refs
        rows, turned, sems = refs[-3:]
        parts = []
        for i in range(0 if inside else n_out):
            for j in range(2):
                some = pl.ds(j * (half // 2), half // 2)
                sem = sems.at[n_moves + len(carried) + 2 * i + j]
                parts.append(pltpu.make_async_copy(outs[i].at[some], out_refs[i].at[some], sem))
        copies = [[], [], []]
        at = 0
        for i, some in enumerate(moves):
            for (_, start, count, side, to, left, right, columns, plane), index in zip(some, where[i]):
                source = row_refs[index].at[pl.ds(start, count), pl.ds(left, columns)]
                into = rows.at[side, pl.ds(to, count), pl.ds(right, columns)]
                copies[plane].append(pltpu.make_async_copy(source, into, sems.at[at]))
                at += 1

        def each(some, do):
            for copy in some:
                do(copy)

        def rows_do(do):
            each(copies[2], do)
            for plane in range(2):
                if copies[plane]:
                    pl.when(place_ref[0] == plane)(lambda plane=plane: each(copies[plane], do))

        rows_do(lambda copy: copy.start())
        if scores:
            pl.when(place_ref[0] == 1)(lambda: each(score_copies, lambda copy: copy.start()))
        rows_do(lambda copy: copy.wait())

        for block in range(2 * per):
            side, column = divmod(block * B, wide)
            turned[block] = rows[side, :, column : column + B].T

        def product(tile):
            right = table_ref[tile, 1]
            return jnp.dot(
                turned[table_ref[tile, 0]],
                rows[right // per, :, pl.ds(pl.multiple_of((right % per) * B, B), B)],
                preferred_element_type=jnp.float32,
            )

        def sibling(tile, _):
            sum_ = product(tile)
            for ref in held[n_own:]:
                sum_ += ref[tile].astype(jnp.float32)
            outs[0][tile] = sum_.astype(outs[0].dtype)
            return 0

        def mine(tile, _):
            sum_ = product(tile + half)
            for ref in held[:n_own]:
                sum_ += ref[tile].astype(jnp.float32)
            if part == "own":
                scale = 1.0 / place_ref[7].astype(jnp.float32)
                sum_ = sum_ * jnp.where(table_ref[tile + half, 2] == 1, scale, 0.0)
            outs[-1][tile] = sum_
            return 0

        if part != "own":
            for j in range(2):
                lax.fori_loop(j * (half // 2), (j + 1) * (half // 2), sibling, 0, unroll=unroll)
                if parts:
                    parts[j].start()
        if part != "sibling":
            for j in range(2):
                lax.fori_loop(j * (half // 2), (j + 1) * (half // 2), mine, 0, unroll=unroll)
                if parts:
                    parts[j - 2].start()
        if scores:

            @pl.when(place_ref[0] == 1)
            def _():
                scores.compute(place_ref, score_outs, *score_scratch[:2], score_copies)

        for copy in parts:
            copy.wait()

    smem = pl.BlockSpec(memory_space=pltpu.SMEM)
    hbm = pl.BlockSpec(memory_space=pltpu.HBM)
    vmem = pl.BlockSpec(memory_space=pltpu.VMEM)
    outs = []
    if part != "own":
        outs.append(jax.ShapeDtypeStruct((half, B, B), jnp.bfloat16))
    if part != "sibling":
        outs.append(jax.ShapeDtypeStruct((half, B, B), jnp.float32))
    return pl.pallas_call(
        kernel,
        out_shape=outs + (scores.out_shape if scores else []),
        in_specs=[smem, smem] + [hbm] * n + [vmem] * len(carried) + [hbm] * len(score_arrays),
        out_specs=[vmem if inside else hbm] * n_out + [pl.BlockSpec(memory_space=pltpu.VMEM)] * n_scores,
        scratch_shapes=[pltpu.VMEM(x.shape, x.dtype) for x in outs if not inside]
        + [
            pltpu.VMEM((2, total, wide), jnp.bfloat16),
            pltpu.VMEM((2 * per, B, total), jnp.bfloat16),
            pltpu.SemaphoreType.DMA((n_moves + len(carried) + 2 * n_out,)),
        ]
        + (scores.scratch if scores else []),
        compiler_params=pltpu.CompilerParams(vmem_limit_bytes=13 * 2**20),
        cost_estimate=pl.CostEstimate(flops=0, bytes_accessed=0, transcendentals=0),
    )(place, table, *arrays, *carried, *score_arrays)


class Scores:
    def __init__(self, parts, slots):
        self.count = [rows_of([slot]) for slot in slots]
        self.moves = []
        for i, slot in enumerate(slots):
            self.moves += plan([slot], sum(self.count[:i]))
        self.quarter = parts[0][0].shape[1]
        lengths = [pair[0].shape[0] for pair in parts]
        self.queries = [x for pair in parts for x in pair]
        self.wide = self.moves[0][0].shape[1]
        self.group = sum(lengths) // 4
        self.arrays = [move[0] for move in self.moves]
        self.out_shape = [
            jax.ShapeDtypeStruct((2, self.group, c), jnp.bfloat16) for c in self.count
        ]
        self.scratch = [
            pltpu.VMEM((2, sum(self.count), self.wide), jnp.bfloat16),
            pltpu.SemaphoreType.DMA((len(self.moves),)),
        ]

    def copies(self, sources, rows, sems):
        out = []
        for i, (_, start, count, side, to, *_) in enumerate(self.moves):
            into = rows.at[side, pl.ds(to, count)]
            out.append(pltpu.make_async_copy(sources[i].at[pl.ds(start, count)], into, sems.at[i]))
        return out

    def compute(self, place_ref, outs, rows, query, copies):
        group, quarter = self.group, self.quarter
        per = self.wide // quarter
        for i, out in enumerate(outs):
            first = sum(self.count[:i])
            for copy, move in zip(copies, self.moves):
                if move[3] < 2 and first <= move[4] < first + self.count[i]:
                    copy.wait()
            for j in range(2):
                total = None
                for k in range(4):
                    spot = place_ref[1 + k]
                    columns = pl.ds(pl.multiple_of((spot % per) * quarter, quarter), quarter)
                    term = lax.dot_general(
                        query[2 * k + j][...],
                        rows[spot // per, first : first + self.count[i], columns],
                        (((1,), (1,)), ((), ())),
                        preferred_element_type=jnp.float32,
                    )
                    total = term if total is None else total + term
                out[j] = total.astype(out.dtype)


def score_call(place, parts, slots):
    scores = Scores(parts, slots)
    n, m = len(slots), len(scores.moves)

    def kernel(place_ref, *refs):
        outs = refs[m + 8 : m + 8 + n]
        rows, sems = refs[m + 8 + n :]

        @pl.when(place_ref[0] == 1)
        def _():
            copies = scores.copies(refs[:m], rows, sems)
            for copy in copies:
                copy.start()
            scores.compute(place_ref, outs, rows, refs[m : m + 8], copies)

    smem = pl.BlockSpec(memory_space=pltpu.SMEM)
    hbm = pl.BlockSpec(memory_space=pltpu.HBM)
    vmem = pl.BlockSpec(memory_space=pltpu.VMEM)
    return pl.pallas_call(
        kernel,
        out_shape=scores.out_shape,
        in_specs=[smem] + [hbm] * m + [vmem] * 8,
        out_specs=[vmem] * n,
        scratch_shapes=scores.scratch,
        compiler_params=pltpu.CompilerParams(vmem_limit_bytes=9 * 2**20),
        cost_estimate=pl.CostEstimate(flops=0, bytes_accessed=0, transcendentals=0),
    )(place, *scores.arrays, *scores.queries)


def weigh_call(place, on_middle, on_ends, swapped, weights):
    group, count = swapped[0].shape

    def kernel(place_ref, *refs):
        late, core = place_ref[5], place_ref[6]
        weight, result, out, sems = refs[6], refs[7], refs[8], refs[9]

        def put(i, block, own_rows):
            row = late if i == 0 else 1 - late
            column = core if own_rows else 1 - core
            across = pl.ds(pl.multiple_of(column * count, count), count)
            down = pl.ds(pl.multiple_of(row * group, group), group)
            out[down, across] = block.astype(jnp.float32) * weight[:, across]

        copies = []
        for i in range(2):
            pl.when(place_ref[0] == 1)(lambda i=i: put(i, refs[i][0], True))
            pl.when(place_ref[0] == 0)(lambda i=i: put(i, refs[2 + i][0], True))
            put(i, refs[4 + i][...], False)
            row = late if i == 0 else 1 - late
            down = pl.ds(pl.multiple_of(row * group, group), group)
            copies.append(pltpu.make_async_copy(out.at[down], result.at[down], sems.at[i]))
            copies[i].start()
        for copy in copies:
            copy.wait()

    smem = pl.BlockSpec(memory_space=pltpu.SMEM)
    vmem = pl.BlockSpec(memory_space=pltpu.VMEM)
    return pl.pallas_call(
        kernel,
        out_shape=jax.ShapeDtypeStruct((2 * group, 2 * count), jnp.float32),
        in_specs=[smem] + [vmem] * 7,
        out_specs=pl.BlockSpec(memory_space=pltpu.HBM),
        scratch_shapes=[
            pltpu.VMEM((2 * group, 2 * count), jnp.float32),
            pltpu.SemaphoreType.DMA((2,)),
        ],
        compiler_params=pltpu.CompilerParams(vmem_limit_bytes=8 * 2**20),
        cost_estimate=pl.CostEstimate(flops=0, bytes_accessed=0, transcendentals=0),
    )(place, *on_middle, *on_ends, *swapped, weights)


def after(values, *done):
    return lax.optimization_barrier(tuple(values) + done)[: len(values)]


def local_line(slab_grads, query_grads, example_weights, tile_owner):
    count, quarter = slab_grads.shape
    half, piece = count // 2, count // 4
    e = lax.axis_index("ex")
    f = lax.axis_index("feat")
    core = f % 2
    middle = jnp.logical_or(e == 1, e == 2)
    late = (e >= 2).astype(jnp.int32)

    def move(value, pairs):
        return lax.ppermute(value, "ex", pairs)

    def across(value):
        return lax.ppermute(value, "feat", ACROSS)

    def swap(value):
        return lax.ppermute(value, "feat", CORE)

    def across_on(value, which):
        pairs = [(p * 4 + g, p * 4 + (g ^ 2)) for p in which for g in range(4)]
        return lax.ppermute(value, ("ex", "feat"), pairs)

    def swap_on(value, which):
        pairs = [(p * 4 + g, p * 4 + (g ^ 1)) for p in which for g in range(4)]
        return lax.ppermute(value, ("ex", "feat"), pairs)

    mids, ends = (1, 2), (0, 3)

    def whole(a, b):
        return ([(a, 0, half)], [(b, 0, half)])

    slots = tile_owner.shape[1] // 4
    own_tiles = lax.dynamic_slice(tile_owner[0], (e * slots, 0), (slots, 2))
    tiles = jnp.concatenate([swap(own_tiles), own_tiles], axis=0)
    blocks = quarter // B
    valid = (tiles[:, :1] >= 0).astype(jnp.int32)
    tiles = jnp.maximum(tiles, 0)
    table = ((tiles // blocks) ^ f) * blocks + tiles % blocks
    table = jnp.concatenate([table, valid], axis=1)
    order = jnp.where(e == 2, jnp.array([2, 3, 1, 0]), jnp.array([1, 0, 2, 3])).astype(jnp.int32)
    place = jnp.concatenate(
        [
            middle.astype(jnp.int32)[None],
            order ^ f,
            late[None],
            core[None],
            jnp.array([4 * count], jnp.int32),
        ]
    )

    give = lax.dynamic_slice(slab_grads, ((1 - core) * half, 0), (half, quarter))
    (slab_grads,) = after((slab_grads,), give)
    keep = lax.dynamic_slice(slab_grads, (core * half, 0), (half, quarter))
    own = jnp.concatenate([keep, swap(give)], axis=1)
    q_half = query_grads.shape[0] // 2

    own_x = across(own)
    near = move(own, PAIR)
    inner = move(own, INNER)

    def halves(value, which):
        return lax.dynamic_slice(value, (which * q_half, 0), (q_half, quarter))

    q_mine, q_other = halves(query_grads, late), halves(query_grads, 1 - late)
    q_mine_sibling = swap(q_mine)
    near, inner, own, own_x, q_mine, q_other, table, q_mine_sibling = after(
        (near, inner, own, own_x, q_mine, q_other, table, q_mine_sibling)
    )
    near_x = across(near)
    outer = move(near, INNER)
    inner_end = move(inner, TO_END)
    q_end_other = move(q_other, TO_MID)
    sibling0, sum0 = tile_call(place, table, whole(own, own_x))

    inner, inner_end, outer, near, near_x, q_end_other, q_mine, sibling0, sum0 = after(
        (inner, inner_end, outer, near, near_x, q_end_other, q_mine, sibling0, sum0)
    )
    second = jnp.where(middle, outer, inner_end)
    second_x = across(second)
    outer_end = move(outer, TO_END)
    q_inner = move(q_other, INNER)
    q_far = move(q_end_other, INNER)
    q_end = move(q_mine, TO_MID)
    sibling1, sum1 = tile_call(place, table, whole(near, near_x), [sum0], sibling0)

    second, second_x, outer_end, inner, sum1, sibling1 = after(
        (second, second_x, outer_end, inner, sum1, sibling1)
    )
    third = jnp.where(middle, inner, outer_end)
    third_x = across(third)
    parts = [(q_mine, q_mine_sibling)] + [(x, swap(x)) for x in (q_end, q_inner, q_far)]
    slots3 = [whole(own, own_x), whole(near, near_x), whole(second, second_x)]
    r_own, r_near, r_outer = score_call(place, parts, slots3)
    far = move(r_outer, INNER)
    to_end = move(r_near, TO_END)
    sibling2, sum2 = tile_call(place, table, whole(second, second_x), [sum1], sibling1)
    third_sibling = swap(third)

    first = jnp.where(middle, r_own[1], to_end[1])
    third_x, to_end, far, sibling2, first = after((third_x, to_end, far, sibling2, first), sum2, r_own)
    first_sibling = swap(first)
    third_x_sibling = swap(third_x)
    (r_inner,) = score_call(place, parts, [whole(third, third_x)])
    sibling2 = swap(sibling2)
    r_inner, far = after((r_inner, far))
    to_far = move(far, TO_END)
    to_mid = move(r_inner, INNER)
    (gram,) = tile_call(
        place,
        table,
        (
            [(third, 0, half), (third_sibling, 0, half, True)],
            [(third_x, 0, half), (third_x_sibling, 0, half, True)],
        ),
        [sum2, sibling2],
        part="own",
    )
    to_end, to_far, to_mid, gram = after((to_end, to_far, to_mid, gram))
    rest_sibling = swap(jnp.where(middle, to_mid[1], to_far[1]))
    scores = weigh_call(
        place,
        (r_own, to_mid),
        (to_end, to_far),
        (first_sibling, rest_sibling),
        example_weights[None, :],
    )
    return gram[None], scores


def solution(mesh):
    placed = (
        P(("grp", "ex"), "feat"),
        P(("grp", "feat"), "ex"),
        P(("grp", "ex")),
        P(("grp", "feat"), None, None),
    )

    line = mesh.shape["ex"] == 4 and mesh.shape["feat"] == 4
    return jax.shard_map(
        local_line if line else local_any,
        mesh=mesh,
        in_specs=placed,
        out_specs=(P(("grp", "feat"), "ex", None, None), P(("grp", "feat"), "ex")),
        check_vma=False,
    )
```
